32 devices in a mesh: frame: 2 (over x), tile: 16 (over z, y, core).
Axes of the slice: x: 2, y: 2, z: 4, core: 2. Of those that a mesh axis runs over, the one named last changes fastest.
Arguments:
- kspace_samples: bfloat16 [4, 64, 32, 128], P('frame', 'tile'), may hold values from -6 to 6
- density: bfloat16 [4, 64, 128], P('frame', 'tile'), may hold values from 0.796875 to 8
- sample_frac: bfloat16 [4, 64, 3, 128], P('frame', 'tile'), may hold values from 0 to 1
- row_offsets: int32 [4, 64, 128], P('frame', 'tile'), may hold values from 0 to 2
- depth_base: int32 [4, 64, 128], P('frame', 'tile'), may hold values from 0 to 127
- block_base: int32 [4, 64, 2], P('frame', 'tile'), may hold values from 0 to 127, as said below
- coil_maps: bfloat16 [16, 2, 128, 128, 128], P(None, None, 'tile'), may hold values from -1.5 to 1.5
- estimate: float32 [4, 2, 128, 128, 128], P('frame', None, 'tile'), may hold values from -6 to 6
Outputs:
- updated: float32 [4, 2, 128, 128, 128], P('frame', None, 'tile')
The draws below stay inside these ranges and needn't reach their ends.
Inputs may be any that keep to these rules, and one draw needn't show every extreme that they name: `block_base`: block b of a frame is held by tile index b // 4. Its kx planes are xb .. xb + 5 mod 128, and tile number p holds planes p * 8 .. p * 8 + 7. In every frame, at most 1 block of one tile index touch any one tile, and some tile is touched by exactly 1 block of every tile index.
All inputs are finite; a program needn't handle non-finite values.
Results may differ from the reference program's by a relative error of at most 0.0095.
Values may be sent and summed in bfloat16 or wider, within the bound.
No kernel may reach another device: no remote copies, remote signals or barrier semaphores. Data moves between devices by JAX's collectives and lax.ppermute only.
A program may use at most 128 MiB of HBM per device.

```python
import math
import jax
import jax.numpy as jnp
from jax import lax

GRID = 128
COILS = 16
BLK_DEV = 4
SAMP = 128
WIN = 8
FRAMES = 4
BLOCKS = 64
CAP = 1
SAMPLES = 8192


def draw_block_base(key, part):
    tile_count = BLOCKS // BLK_DEV
    tile_width = GRID // tile_count
    centre_span = 1 + (tile_width + 4) // tile_width
    region = (tile_count - centre_span) // 3
    key_centre, key_near, key_far, key_rows = jax.random.split(key, 4)
    centre = jax.random.randint(key_centre, (FRAMES, 1), 0, tile_count)
    local_block = jnp.arange(BLOCKS).astype(jnp.int32) % BLK_DEV
    group = (local_block // CAP)[None, :]
    near_plane = centre * tile_width + jax.random.randint(key_near, (FRAMES, BLOCKS), 0, tile_width)
    region_first = (centre + centre_span + (group - 1) * region) * tile_width
    far_plane = region_first + jax.random.randint(key_far, (FRAMES, BLOCKS), 0, region * tile_width - 5)
    plane = jnp.where(group == 0, near_plane, far_plane) % GRID
    row_first = jax.random.randint(key_rows, (FRAMES, BLOCKS), 0, GRID)
    return jnp.stack([plane, row_first], axis=-1).astype(jnp.int32)


def set_ends(values, rng, smallest, high):
    index_at = [jax.random.randint(jax.random.fold_in(rng, axis), (), 0, length) for axis, length in enumerate(values.shape)]
    widest = values.shape.index(max(values.shape))
    next_to = index_at[:widest] + [(index_at[widest] + 1) % values.shape[widest]] + index_at[widest + 1:]
    return values.at[tuple(index_at)].set(smallest).at[tuple(next_to)].set(high)


def steps_of(own_key, shape, pieces, low, high):
    def one(axis_at, blocks):
        heights = jax.random.uniform(jax.random.fold_in(jax.random.fold_in(own_key, 6), axis_at), (blocks,), jnp.float32, low / len(pieces), high / len(pieces))
        return jnp.repeat(jnp.exp(heights), shape[axis_at] // blocks).reshape((-1,) + (1,) * (len(shape) - axis_at - 1))

    loudness = one(*pieces[0])
    for cut in pieces[1:]:
        loudness = loudness * one(*cut)
    return loudness


def normal_values(stream_key, shape, deviation, limit, shards=(), kind=jnp.bfloat16):
    level = steps_of(stream_key, shape, shards, -0.22, 0.18) if shards else 1.0
    entries = jax.random.normal(stream_key, shape, jnp.float32) * deviation * level
    return jnp.minimum(jnp.maximum(entries, -limit), limit).astype(kind)


def setup_inputs(seed: int = 0) -> dict:
    splits = jax.random.split(jax.random.key(seed), 9)
    kspace_samples = normal_values(splits[0], (FRAMES, BLOCKS, 2 * COILS, SAMP), 1.0, 6.0, ((0, 2), (1, 16)))
    density = jnp.clip(jnp.exp(math.log(8.0) - 2.306499 * jax.random.uniform(splits[1], (FRAMES, BLOCKS, SAMP), jnp.float32) ** steps_of(splits[1], (FRAMES, BLOCKS, SAMP), ((0, 2), (1, 16)), -0.2, 0.2)), 0.796875, 8.0).astype(jnp.bfloat16)
    sample_frac = jnp.clip(1.0 * jax.random.uniform(splits[2], (FRAMES, BLOCKS, 3, SAMP), jnp.float32) ** steps_of(splits[2], (FRAMES, BLOCKS, 3, SAMP), ((0, 2), (1, 16)), -0.2, 0.2), 0.0, 1.0).astype(jnp.bfloat16)
    row_offsets = set_ends(jax.random.randint(splits[3], (FRAMES, BLOCKS, SAMP), 0, WIN - 5), jax.random.fold_in(splits[3], 1), 0, (WIN - 5) - 1).astype(jnp.int32)
    depth_base = set_ends(jax.random.randint(splits[4], (FRAMES, BLOCKS, SAMP), 0, GRID), jax.random.fold_in(splits[4], 1), 0, GRID - 1).astype(jnp.int32)
    block_base = draw_block_base(jax.random.fold_in(splits[8], 71), 0)
    coil_maps = normal_values(splits[6], (COILS, 2, GRID, GRID, GRID), 0.25, 1.5, ((2, 16),))
    estimate = normal_values(splits[7], (FRAMES, 2, GRID, GRID, GRID), 1.0, 6.0, ((0, 2), (2, 16)), jnp.float32)
    return {"kspace_samples": kspace_samples, "density": density, "sample_frac": sample_frac, "row_offsets": row_offsets, "depth_base": depth_base, "block_base": block_base, "coil_maps": coil_maps, "estimate": estimate}


BETA = 13.9
EPS = 0.05
LAMBDA_TV = 0.3

def bessel_zero(argument):
    quarter = argument * argument / 4.0
    series_term = jnp.ones_like(argument)
    series_sum = jnp.ones_like(argument)
    for power in range(1, 40):
        series_term = series_term * quarter / float(power * power)
        series_sum = series_sum + series_term
    return series_sum

def kaiser(offset, fraction):
    distance = offset.astype(jnp.float32) - 2.0 - fraction
    inside = jnp.maximum(1.0 - distance / 3.0 * (distance / 3.0), 0.0)
    return bessel_zero(BETA * jnp.sqrt(inside)) / bessel_zero(jnp.full_like(distance, BETA))

def to_bfloat(values):
    return lax.optimization_barrier(values.astype(jnp.bfloat16)).astype(jnp.float32)

def inverse_pass(real_part, imag_part, axis_pos):
    field = lax.complex(real_part, imag_part)
    result = jnp.fft.ifft(field, axis=axis_pos) * GRID
    return (jnp.real(result), jnp.imag(result))

def reference(kspace_samples, density, sample_frac, row_offsets, depth_base, block_base, coil_maps, estimate):
    scale = 1.0 / (8.0 * math.sqrt(SAMPLES))
    offsets = jnp.arange(6).astype(jnp.int32)
    maps_real = jnp.moveaxis(coil_maps[:, 0].astype(jnp.float32), 0, -1)
    maps_imag = jnp.moveaxis(coil_maps[:, 1].astype(jnp.float32), 0, -1)

    def one_frame(inputs):
        samples, weights, fractions, row_shift, depth_start, block_start = inputs
        channels = samples.shape[1]
        frac_x = fractions[:, 0].astype(jnp.float32)
        frac_y = fractions[:, 1].astype(jnp.float32)
        frac_z = fractions[:, 2].astype(jnp.float32)
        along_x = kaiser(offsets[:, None, None], frac_x[None])
        along_y = kaiser(offsets[:, None, None], frac_y[None])
        along_z = to_bfloat(kaiser(offsets[:, None, None], frac_z[None]))
        amplitude = weights.astype(jnp.float32)[:, :, None] * jnp.swapaxes(samples, 1, 2).astype(jnp.float32)
        row_first = block_start[:, 1][:, None] + row_shift
        y_pos = (row_first[None] + offsets[:, None, None]) % GRID
        z_pos = (depth_start[None] + offsets[:, None, None]) % GRID
        cells = jnp.zeros((GRID * GRID * GRID, channels), jnp.float32)
        for tap_index in range(6):
            x_pos = (block_start[:, 0] + tap_index) % GRID
            outer = to_bfloat(amplitude[None] * along_x[tap_index][None, :, :, None] * along_y[:, :, :, None])
            values = outer[:, None] * along_z[None, :, :, :, None]
            flat = (y_pos[:, None] * GRID + x_pos[None, None, :, None]) * GRID + z_pos[None]
            cells = cells.at[flat.reshape(-1).astype(jnp.int32)].add(values.reshape(-1, channels))
        kspace = to_bfloat(cells).reshape(GRID, GRID, GRID, channels // 2, 2)
        real_part, imag_part = inverse_pass(kspace[..., 0], kspace[..., 1], 0)
        real_part, imag_part = (to_bfloat(real_part), to_bfloat(imag_part))
        real_part, imag_part = inverse_pass(real_part, imag_part, 2)
        real_part, imag_part = (to_bfloat(real_part), to_bfloat(imag_part))
        real_part, imag_part = inverse_pass(real_part, imag_part, 1)
        back_real = scale * lax.optimization_barrier(jnp.sum(maps_real * real_part + maps_imag * imag_part, axis=-1))
        back_imag = scale * lax.optimization_barrier(jnp.sum(maps_real * imag_part - maps_imag * real_part, axis=-1))
        return jnp.stack([back_real, back_imag], axis=0)
    back = lax.map(one_frame, (kspace_samples, density, sample_frac, row_offsets, depth_base, block_base))
    half = estimate + back
    change = half[1:] - half[:-1]
    magnitude = jnp.sqrt(change[:, 0] * change[:, 0] + change[:, 1] * change[:, 1] + EPS * EPS)
    psi = change / magnitude[:, None]
    zero_frame = jnp.zeros_like(psi[:1])
    psi_before = jnp.concatenate([zero_frame, psi], axis=0)
    psi_after = jnp.concatenate([psi, zero_frame], axis=0)
    return half - LAMBDA_TV * (psi_before - psi_after)
```

```python
import functools
import math

import jax
import jax.numpy as jnp
import numpy as np
from jax import lax
from jax.experimental import pallas as pl
from jax.experimental.pallas import tpu as pltpu
from jax.sharding import PartitionSpec as P

TAPS = 6
WIN = 8
YROWS = 8
META = 8
BETA = 13.9
EPS = 0.05
LAMBDA_TV = 0.3
TERMS = 40
VMEM_LIMIT = 56 * 1024 * 1024


def kaiser_coefficients():
    quarter = BETA * BETA / 4.0
    terms = [quarter**power / math.factorial(power) ** 2 for power in range(TERMS)]
    total = math.fsum(terms)
    return [term / total for term in terms]


def kaiser(distance):
    coefficients = kaiser_coefficients()
    inside = jnp.maximum(1.0 - distance / 3.0 * (distance / 3.0), 0.0)
    value = jnp.full_like(inside, coefficients[-1])
    for coefficient in coefficients[-2::-1]:
        value = value * inside + coefficient
    return value


def dft_angles(grid_size):
    positions = np.arange(grid_size)
    return (positions[:, None] * positions[None, :] % grid_size) * (2.0 * math.pi / grid_size)


def depth_table(grid_size):
    angles = dft_angles(grid_size)
    return jnp.asarray(np.concatenate([np.cos(angles), np.sin(angles)], axis=0), jnp.bfloat16)


def plane_table(grid_size):
    angles = dft_angles(grid_size)
    cosine, sine = np.cos(angles), np.sin(angles)
    return jnp.asarray(np.block([[cosine, -sine], [sine, cosine]]), jnp.bfloat16)


def row_tables(grid_size, first_row):
    rows = jnp.arange(grid_size + WIN)[:, None] * (first_row + jnp.arange(YROWS))[None, :]
    angles = (rows % grid_size).astype(jnp.float32) * (2.0 * math.pi / grid_size)
    shape = (grid_size + WIN, YROWS, 128)
    return (
        jnp.broadcast_to(jnp.cos(angles)[:, :, None], shape),
        jnp.broadcast_to(jnp.sin(angles)[:, :, None], shape),
    )


def frame_kernel(
    corner, own, other, cos_rows, sin_rows, depth_dft, plane_dft, maps_hbm, estimate_hbm,
    half, half_small,
    grid_real, grid_imag, weights, weight_x, weight_y, maps, estimate, sems,
    *, scale,
):
    blocks = own.shape[0]
    samples = own.shape[2]
    coils, _, slab, grid_size, _ = maps.shape
    plane_rows = coils * YROWS
    copies = [
        pltpu.make_async_copy(maps_hbm, maps, sems.at[0]),
        pltpu.make_async_copy(estimate_hbm.at[corner[0]], estimate, sems.at[1]),
    ]
    for copy in copies:
        copy.start()

    def clear(step, carry):
        zeros = jnp.zeros((plane_rows, 128), jnp.float32)
        at = pl.ds(pl.multiple_of(step * plane_rows, plane_rows), plane_rows)
        grid_real[at, :] = zeros
        grid_imag[at, :] = zeros
        return carry

    lax.fori_loop(0, grid_size + WIN, clear, 0)

    table = depth_dft[...]
    taps = lax.broadcasted_iota(jnp.int32, (8, samples), 0).astype(jnp.float32)
    cells = lax.broadcasted_iota(jnp.int32, (grid_size, samples), 0)

    def prepare(source, offset):
        def one(block):
            meta = source[block].astype(jnp.float32)[2 * coils :]
            density, frac_x, frac_y, frac_z, shift, depth = (meta[row : row + 1] for row in range(6))
            weight_x[offset + block] = kaiser(taps - 2.0 - frac_x) * density
            lag = taps - shift
            weight_y[offset + block] = jnp.where(
                (lag >= 0.0) & (lag < float(TAPS)), kaiser(lag - 2.0 - frac_y), 0.0
            )
            tap_z = kaiser(taps - 2.0 - frac_z)
            lag_z = (cells - depth.astype(jnp.int32)) & (grid_size - 1)
            spread = jnp.zeros((grid_size, samples), jnp.float32)
            for tap in range(TAPS):
                spread = jnp.where(lag_z == tap, tap_z[tap : tap + 1], spread)
            turned = jnp.dot(
                table, spread.astype(jnp.bfloat16), preferred_element_type=jnp.float32
            ).astype(jnp.bfloat16)
            real, imag = turned[:grid_size], turned[grid_size:]
            weights[offset + block, :, :samples] = turned
            weights[offset + block, :grid_size, samples:] = -imag
            weights[offset + block, grid_size:, samples:] = real

        def step(index, carry):
            for part in range(2):
                one(index * 2 + part)
            return carry

        lax.fori_loop(0, blocks // 2, step, 0)

    prepare(own, 0)
    prepare(other, blocks)

    def spread_planes(source, offset):
        def one(block):
            first_plane = corner[1 + 2 * (offset + block)]
            first_row = corner[2 + 2 * (offset + block)]
            payload = source[block].astype(jnp.float32)
            row_weights = weight_y[offset + block]
            turn_real = jnp.zeros((YROWS, samples), jnp.float32)
            turn_imag = jnp.zeros((YROWS, samples), jnp.float32)
            for row in range(WIN):
                weight = row_weights[row : row + 1]
                turn_real = turn_real + cos_rows[first_row + row] * weight
                turn_imag = turn_imag + sin_rows[first_row + row] * weight
            real, imag = [], []
            for coil in range(coils):
                amp_real = payload[2 * coil : 2 * coil + 1]
                amp_imag = payload[2 * coil + 1 : 2 * coil + 2]
                real.append(amp_real * turn_real - amp_imag * turn_imag)
                imag.append(amp_real * turn_imag + amp_imag * turn_real)
            amplitude = jnp.concatenate(
                [jnp.concatenate(real, axis=0), jnp.concatenate(imag, axis=0)], axis=1
            )
            plane_weights = weight_x[offset + block]
            plane_weights = jnp.concatenate([plane_weights, plane_weights], axis=1)
            depth_weights = weights[offset + block]
            base = first_plane * plane_rows
            for tap in range(TAPS):
                left = (amplitude * plane_weights[tap : tap + 1]).astype(jnp.bfloat16)
                product = lax.dot_general(
                    left, depth_weights, (((1,), (1,)), ((), ())),
                    preferred_element_type=jnp.float32,
                )
                at = pl.ds(pl.multiple_of(base + tap * plane_rows, plane_rows), plane_rows)
                grid_real[at, :] = grid_real[at, :] + product[:, :grid_size]
                grid_imag[at, :] = grid_imag[at, :] + product[:, grid_size:]

        def step(index, carry):
            for part in range(2):
                one(index * 2 + part)
            return carry

        lax.fori_loop(0, blocks // 2, step, 0)

    spread_planes(own, 0)
    spread_planes(other, blocks)

    wrap = (TAPS - 1) * plane_rows
    for ref in (grid_real, grid_imag):
        ref[:wrap, :] = ref[:wrap, :] + ref[grid_size * plane_rows : grid_size * plane_rows + wrap, :]

    for copy in copies:
        copy.wait()
    plane_matrix = plane_dft[...]

    def image_row(row, carry):
        total_real = jnp.zeros((grid_size, grid_size), jnp.float32)
        total_imag = jnp.zeros((grid_size, grid_size), jnp.float32)
        for pair in range(coils // 2):
            columns = []
            for coil in (2 * pair, 2 * pair + 1):
                at = pl.ds(coil * YROWS + row, grid_size, stride=plane_rows)
                columns.append(jnp.concatenate(
                    [grid_real[at, :].astype(jnp.bfloat16), grid_imag[at, :].astype(jnp.bfloat16)],
                    axis=0,
                ))
            images = jnp.dot(
                plane_matrix, jnp.concatenate(columns, axis=1), preferred_element_type=jnp.float32
            )
            for place, coil in enumerate((2 * pair, 2 * pair + 1)):
                image = images[:, place * grid_size : (place + 1) * grid_size]
                image_real, image_imag = image[:grid_size], image[grid_size:]
                map_real = maps[coil, 0, row].astype(jnp.float32)
                map_imag = maps[coil, 1, row].astype(jnp.float32)
                total_real = total_real + (map_real * image_real + map_imag * image_imag)
                total_imag = total_imag + (map_real * image_imag - map_imag * image_real)
        for part, total in enumerate((total_real, total_imag)):
            value = estimate[part, row] + scale * total
            half[part, row] = value
            half_small[part, row] = value.astype(jnp.bfloat16)
        return carry

    lax.fori_loop(0, slab, image_row, 0)


def frame_image(corner, own, other, tables, coil_maps, estimate, scale):
    blocks, _, samples = own.shape
    coils, _, slab, grid_size, _ = coil_maps.shape
    shape = (2, slab, grid_size, grid_size)
    whole = pl.BlockSpec(memory_space=pltpu.VMEM)
    away = pl.BlockSpec(memory_space=pl.ANY)
    grid_shape = ((grid_size + WIN) * coils * YROWS, grid_size)
    return pl.pallas_call(
        functools.partial(frame_kernel, scale=scale),
        out_shape=(
            jax.ShapeDtypeStruct(shape, jnp.float32),
            jax.ShapeDtypeStruct(shape, jnp.bfloat16),
        ),
        in_specs=[pl.BlockSpec(memory_space=pltpu.SMEM)] + [whole] * 6 + [away] * 2,
        out_specs=(whole, whole),
        scratch_shapes=[
            pltpu.VMEM(grid_shape, jnp.float32),
            pltpu.VMEM(grid_shape, jnp.float32),
            pltpu.VMEM((2 * blocks, 2 * grid_size, 2 * samples), jnp.bfloat16),
            pltpu.VMEM((2 * blocks, 8, samples), jnp.float32),
            pltpu.VMEM((2 * blocks, 8, samples), jnp.float32),
            pltpu.VMEM(coil_maps.shape, jnp.bfloat16),
            pltpu.VMEM(shape, jnp.float32),
            pltpu.SemaphoreType.DMA((2,)),
        ],
        compiler_params=pltpu.CompilerParams(vmem_limit_bytes=VMEM_LIMIT),
        cost_estimate=pl.CostEstimate(
            flops=2 * 2 * blocks * TAPS * coils * YROWS * 4 * samples * grid_size,
            bytes_accessed=coil_maps.size * 2,
            transcendentals=0,
        ),
    )(corner, own, other, *tables, coil_maps, estimate)


def swap(values, axis, bit):
    count = lax.axis_size(axis)
    return lax.ppermute(values, axis, [(index, index ^ bit) for index in range(count)])


def gather_blocks(packed):
    count = lax.axis_size("tile")
    held = packed[None]
    bits = [1 << place for place in range(1, count.bit_length() - 1)]
    for bit in reversed(bits):
        held = jnp.concatenate([held, swap(held, "tile", bit)], axis=0)
    held = held.reshape((-1,) + packed.shape[1:])
    return held, swap(held, "tile", 1)


def on_device(
    kspace_samples, density, sample_frac, row_offsets, depth_base, block_base, coil_maps, estimate
):
    tile_count = lax.axis_size("tile")
    tile_here = lax.axis_index("tile")
    frame_count = lax.axis_size("frame")
    frame_here = lax.axis_index("frame")
    frames_local, blocks_local, channels, sample_count = kspace_samples.shape
    grid_size = coil_maps.shape[3]
    slab = coil_maps.shape[2]
    scale = 1.0 / (8.0 * math.sqrt(blocks_local * tile_count * sample_count))
    last = frames_local - 1

    corner_rows = jnp.broadcast_to(
        block_base.astype(jnp.bfloat16)[..., None], block_base.shape + (sample_count,)
    )
    packed = jnp.concatenate(
        [
            kspace_samples,
            density[:, :, None],
            sample_frac,
            row_offsets.astype(jnp.bfloat16)[:, :, None],
            depth_base.astype(jnp.bfloat16)[:, :, None],
            corner_rows,
        ],
        axis=2,
    )
    tables = row_tables(grid_size, tile_here * slab) + (
        depth_table(grid_size), plane_table(grid_size),
    )
    even = frame_here % 2 == 0
    order = [jnp.where(even, last, 0), jnp.where(even, 0, last)]

    halves, received = [], []
    for place, frame in enumerate(order):
        own, other = gather_blocks(lax.dynamic_index_in_dim(packed, frame, 0, keepdims=False))
        corner = jnp.concatenate([own[:, -2:, 0], other[:, -2:, 0]], axis=0)
        corner = jnp.concatenate([frame[None].astype(jnp.int32), corner.reshape(-1).astype(jnp.int32)])
        half, small = frame_image(corner, own, other, tables, coil_maps, estimate, scale)
        halves.append(half)
        if place == 0:
            pairs = [(index, index ^ 1) for index in range(frame_count) if index ^ 1 < frame_count]
        else:
            pairs = [(index, index - 1) for index in range(2, frame_count, 2)]
            pairs += [(target, source) for source, target in pairs]
        received.append(lax.ppermute(small, "frame", pairs) if pairs else jnp.zeros_like(small))

    first = jnp.where(even, halves[1], halves[0])
    second = jnp.where(even, halves[0], halves[1])
    before = jnp.where(even, received[1], received[0]).astype(jnp.float32)
    after = jnp.where(even, received[0], received[1]).astype(jnp.float32)

    def psi(low, high):
        change = high - low
        return change / jnp.sqrt(
            change[0] * change[0] + change[1] * change[1] + EPS * EPS
        )[None]

    middle = psi(first, second)
    low = jnp.where(frame_here > 0, psi(before, first), 0.0)
    high = jnp.where(frame_here < frame_count - 1, psi(second, after), 0.0)
    return jnp.stack(
        [first - LAMBDA_TV * (low - middle), second - LAMBDA_TV * (middle - high)], axis=0
    )


def solution(mesh):
    in_specs = (
        P("frame", "tile", None, None),
        P("frame", "tile", None),
        P("frame", "tile", None, None),
        P("frame", "tile", None),
        P("frame", "tile", None),
        P("frame", "tile", None),
        P(None, None, "tile", None, None),
        P("frame", None, "tile", None, None),
    )
    out_specs = P("frame", None, "tile", None, None)
    return jax.shard_map(
        on_device, mesh=mesh, in_specs=in_specs, out_specs=out_specs, check_vma=False
    )
```

```python
import functools
import math

import jax
import jax.numpy as jnp
import numpy as np
from jax import lax
from jax.experimental import pallas as pl
from jax.experimental.pallas import tpu as pltpu
from jax.sharding import PartitionSpec as P

TAPS = 6
WIN = 8
YROWS = 8
META = 8
BETA = 13.9
EPS = 0.05
LAMBDA_TV = 0.3
TERMS = 40
UNROLL = 8
VMEM_LIMIT = 56 * 1024 * 1024


def kaiser_coefficients():
    quarter = BETA * BETA / 4.0
    terms = [quarter**power / math.factorial(power) ** 2 for power in range(TERMS)]
    total = math.fsum(terms)
    return [term / total for term in terms]


def kaiser(distance):
    coefficients = kaiser_coefficients()
    inside = jnp.maximum(1.0 - distance / 3.0 * (distance / 3.0), 0.0)
    value = jnp.full_like(inside, coefficients[-1])
    for coefficient in coefficients[-2::-1]:
        value = value * inside + coefficient
    return value


def dft_angles(grid_size):
    positions = np.arange(grid_size)
    return (positions[:, None] * positions[None, :] % grid_size) * (2.0 * math.pi / grid_size)


def depth_table(grid_size):
    angles = dft_angles(grid_size)
    return jnp.asarray(np.concatenate([np.cos(angles), np.sin(angles)], axis=0), jnp.bfloat16)


def plane_table(grid_size):
    angles = dft_angles(grid_size)
    cosine, sine = np.cos(angles), np.sin(angles)
    parts = np.stack([np.concatenate([cosine, -sine], 1), np.concatenate([sine, cosine], 1)])
    tiles = parts.reshape(2, grid_size // 8, 8, 2 * grid_size).swapaxes(0, 1)
    return jnp.asarray(tiles.reshape(2 * grid_size, 2 * grid_size), jnp.bfloat16)


def row_tables(grid_size, first_row):
    rows = jnp.arange(grid_size + WIN)[:, None] * (first_row + jnp.arange(YROWS))[None, :]
    angles = (rows % grid_size).astype(jnp.float32) * (2.0 * math.pi / grid_size)
    shape = (grid_size + WIN, YROWS, 128)
    return (
        jnp.broadcast_to(jnp.cos(angles)[:, :, None], shape),
        jnp.broadcast_to(jnp.sin(angles)[:, :, None], shape),
    )


def frame_kernel(
    corner, own, other, cos_rows, sin_rows, depth_dft, plane_dft, maps_hbm, estimate_hbm,
    half, half_small,
    grid_real, grid_imag, left, weights, weight_x, weight_y, columns, maps, estimate, total, sems,
    *, scale,
):
    blocks = own.shape[0]
    samples = own.shape[2]
    unroll = len(left)
    coils, _, slab, grid_size, _ = maps.shape
    copies = [
        pltpu.make_async_copy(maps_hbm, maps, sems.at[0]),
        pltpu.make_async_copy(estimate_hbm.at[corner[0]], estimate, sems.at[1]),
    ]
    for copy in copies:
        copy.start()

    table = depth_dft[...]
    taps = lax.broadcasted_iota(jnp.int32, (8, 2 * samples), 0).astype(jnp.float32)
    cells = lax.broadcasted_iota(jnp.int32, (grid_size, 2 * samples), 0).astype(jnp.bfloat16)
    clear_rows = grid_real[0].shape[0] // (blocks // unroll)

    def prepare(source, offset, cleared):
        def two(first):
            meta = jnp.concatenate(
                [source[first + part].astype(jnp.float32)[2 * coils :] for part in range(2)], axis=1
            )
            density, frac_x, frac_y, frac_z, shift, depth = (meta[row : row + 1] for row in range(6))
            tap_x = kaiser(taps - 2.0 - frac_x) * density
            lag = taps - shift
            tap_y = jnp.where((lag >= 0.0) & (lag < float(TAPS)), kaiser(lag - 2.0 - frac_y), 0.0)
            tap_z = kaiser(taps - 2.0 - frac_z).astype(jnp.bfloat16)
            cell = depth + taps
            cell = jnp.where(cell >= float(grid_size), cell - float(grid_size), cell)
            cell = cell.astype(jnp.bfloat16)
            spread = jnp.zeros((grid_size, 2 * samples), jnp.bfloat16)
            for tap in range(TAPS):
                spread = jnp.where(cells == cell[tap : tap + 1], tap_z[tap : tap + 1], spread)
            turned = jnp.dot(table, spread, preferred_element_type=jnp.float32).astype(jnp.bfloat16)
            real, imag = turned[:grid_size], turned[grid_size:]
            for part in range(2):
                at, here = offset + first + part, slice(part * samples, (part + 1) * samples)
                weight_x[at] = tap_x[:, here]
                weight_y[at] = tap_y[:, here]
                weights[at, :, :samples] = turned[:, here]
                weights[at, :grid_size, samples:] = -imag[:, here]
                weights[at, grid_size:, samples:] = real[:, here]

        def step(index, carry):
            for ref in cleared:
                at = pl.ds(pl.multiple_of(index * clear_rows, 8), clear_rows)
                ref[at, :] = jnp.zeros((clear_rows, grid_size), jnp.float32)
            for part in range(0, unroll, 2):
                two(index * unroll + part)
            return carry

        lax.fori_loop(0, blocks // unroll, step, 0)

    prepare(own, 0, grid_real)
    prepare(other, blocks, grid_imag)

    def build(source, offset, block, slot):
        first_row = corner[2 + 2 * (offset + block)]
        payload = source[block].astype(jnp.float32)
        row_weights = weight_y[offset + block]
        plane_weights = weight_x[offset + block]
        turn_real = jnp.zeros((YROWS, samples), jnp.float32)
        turn_imag = jnp.zeros((YROWS, samples), jnp.float32)
        for row in range(WIN):
            weight = row_weights[row : row + 1]
            turn_real = turn_real + cos_rows[first_row + row] * weight
            turn_imag = turn_imag + sin_rows[first_row + row] * weight
        by_plane = []
        for tap in range(0, TAPS, 2):
            by_plane.append(jnp.concatenate(
                [jnp.broadcast_to(plane_weights[at : at + 1], (YROWS, samples)) for at in (tap, tap + 1)],
                axis=0,
            ).astype(jnp.bfloat16))
        for coil in range(coils):
            amp_real = payload[2 * coil : 2 * coil + 1]
            amp_imag = payload[2 * coil + 1 : 2 * coil + 2]
            parts = (
                amp_real * turn_real - amp_imag * turn_imag,
                amp_real * turn_imag + amp_imag * turn_real,
            )
            for part, value in enumerate(parts):
                twice = jnp.concatenate([value, value], axis=0).astype(jnp.bfloat16)
                for pair, weight in enumerate(by_plane):
                    left[slot][
                        pl.ds(coil * TAPS * YROWS + pair * 2 * YROWS, 2 * YROWS),
                        pl.ds(part * samples, samples),
                    ] = twice * weight

    def spread(offset, block, slot):
        first_plane = corner[1 + 2 * (offset + block)]
        product = lax.dot_general(
            left[slot][...], weights[offset + block], (((1,), (1,)), ((), ())),
            preferred_element_type=jnp.float32,
        )
        rows = TAPS * YROWS
        for coil in range(coils):
            at = pl.ds(pl.multiple_of(first_plane * YROWS, YROWS), rows)
            part = product[coil * rows : (coil + 1) * rows]
            grid_real[coil][at, :] = grid_real[coil][at, :] + part[:, :grid_size]
            grid_imag[coil][at, :] = grid_imag[coil][at, :] + part[:, grid_size:]

    def spread_planes(source, offset):
        build(source, offset, 0, 0)

        def step(index, carry):
            block = index * unroll
            for part in range(unroll):
                later = jnp.minimum(block + part + 1, blocks - 1)
                build(source, offset, later, (part + 1) % unroll)
                spread(offset, block + part, part)
            return carry

        lax.fori_loop(0, blocks // unroll, step, 0)

    spread_planes(own, 0)
    spread_planes(other, blocks)

    wrap = (TAPS - 1) * YROWS
    top = grid_size * YROWS
    for ref in grid_real + grid_imag:
        ref[:wrap, :] = ref[:wrap, :] + ref[top : top + wrap, :]

    for copy in copies:
        copy.wait()

    def transpose(row, slot):
        at = pl.ds(row, grid_size, stride=YROWS)
        for coil in range(coils):
            lanes = pl.ds((coil % 2) * grid_size, grid_size)
            columns[slot][coil // 2, :grid_size, lanes] = grid_real[coil][at, :].astype(jnp.bfloat16)
            columns[slot][coil // 2, grid_size:, lanes] = grid_imag[coil][at, :].astype(jnp.bfloat16)

    def image_row(row, slot):
        for quad in range(coils // 4):
            images = [
                jnp.dot(plane_dft[...], columns[slot][pair], preferred_element_type=jnp.float32)
                for pair in (2 * quad, 2 * quad + 1)
            ]
            for tile in range(grid_size // 16):
                sums = [[], []]
                for place in range(4):
                    coil = 4 * quad + place
                    column = (place % 2) * grid_size
                    image = images[place // 2][tile * 32 : tile * 32 + 32, column : column + grid_size]
                    image_real = jnp.concatenate([image[:8], image[16:24]], axis=0)
                    image_imag = jnp.concatenate([image[8:16], image[24:]], axis=0)
                    map_real = maps[coil, 0, row, pl.ds(tile * 16, 16)].astype(jnp.float32)
                    map_imag = maps[coil, 1, row, pl.ds(tile * 16, 16)].astype(jnp.float32)
                    sums[0].append(map_real * image_real + map_imag * image_imag)
                    sums[1].append(map_real * image_imag - map_imag * image_real)
                at = pl.ds(tile * 16, 16)
                for part in range(2):
                    value = (sums[part][0] + sums[part][1]) + (sums[part][2] + sums[part][3])
                    if quad > 0:
                        value = value + total[part, at]
                    if quad < coils // 4 - 1:
                        total[part, at] = value
                    else:
                        value = estimate[part, row, at] + scale * value
                        half[part, row, at] = value
                        half_small[part, row, at] = value.astype(jnp.bfloat16)

    transpose(0, 0)

    def two_rows(index, carry):
        row = 2 * index
        transpose(row + 1, 1)
        image_row(row, 0)
        transpose(jnp.minimum(row + 2, slab - 1), 0)
        image_row(row + 1, 1)
        return carry

    lax.fori_loop(0, slab // 2, two_rows, 0)


def frame_image(corner, own, other, tables, coil_maps, estimate, scale):
    blocks, _, samples = own.shape
    coils, _, slab, grid_size, _ = coil_maps.shape
    shape = (2, slab, grid_size, grid_size)
    whole = pl.BlockSpec(memory_space=pltpu.VMEM)
    away = pl.BlockSpec(memory_space=pl.ANY)
    grid_shape = ((grid_size + WIN) * YROWS, grid_size)
    return pl.pallas_call(
        functools.partial(frame_kernel, scale=scale),
        out_shape=(
            jax.ShapeDtypeStruct(shape, jnp.float32),
            jax.ShapeDtypeStruct(shape, jnp.bfloat16),
        ),
        in_specs=[pl.BlockSpec(memory_space=pltpu.SMEM)] + [whole] * 6 + [away] * 2,
        out_specs=(whole, whole),
        scratch_shapes=[
            [pltpu.VMEM(grid_shape, jnp.float32)] * coils,
            [pltpu.VMEM(grid_shape, jnp.float32)] * coils,
            [pltpu.VMEM((coils * TAPS * YROWS, 2 * samples), jnp.bfloat16)] * math.gcd(blocks, UNROLL),
            pltpu.VMEM((2 * blocks, 2 * grid_size, 2 * samples), jnp.bfloat16),
            pltpu.VMEM((2 * blocks, 8, samples), jnp.float32),
            pltpu.VMEM((2 * blocks, 8, samples), jnp.float32),
            [pltpu.VMEM((coils // 2, 2 * grid_size, 2 * grid_size), jnp.bfloat16)] * 2,
            pltpu.VMEM(coil_maps.shape, jnp.bfloat16),
            pltpu.VMEM(shape, jnp.float32),
            pltpu.VMEM((2, grid_size, grid_size), jnp.float32),
            pltpu.SemaphoreType.DMA((2,)),
        ],
        compiler_params=pltpu.CompilerParams(vmem_limit_bytes=VMEM_LIMIT),
        cost_estimate=pl.CostEstimate(
            flops=2 * 2 * blocks * TAPS * coils * YROWS * 4 * samples * grid_size,
            bytes_accessed=coil_maps.size * 2,
            transcendentals=0,
        ),
    )(corner, own, other, *tables, coil_maps, estimate)


def swap(values, axis, bit):
    count = lax.axis_size(axis)
    return lax.ppermute(values, axis, [(index, index ^ bit) for index in range(count)])


def gather_blocks(packed):
    count = lax.axis_size("tile")
    held = packed[None]
    bits = [1 << place for place in range(1, count.bit_length() - 1)]
    for bit in reversed(bits):
        held = jnp.concatenate([held, swap(held, "tile", bit)], axis=0)
    held = held.reshape((-1,) + packed.shape[1:])
    return held, swap(held, "tile", 1)


def on_device(
    kspace_samples, density, sample_frac, row_offsets, depth_base, block_base, coil_maps, estimate
):
    tile_count = lax.axis_size("tile")
    tile_here = lax.axis_index("tile")
    frame_count = lax.axis_size("frame")
    frame_here = lax.axis_index("frame")
    frames_local, blocks_local, channels, sample_count = kspace_samples.shape
    grid_size = coil_maps.shape[3]
    slab = coil_maps.shape[2]
    scale = 1.0 / (8.0 * math.sqrt(blocks_local * tile_count * sample_count))
    last = frames_local - 1

    corner_rows = jnp.broadcast_to(
        block_base.astype(jnp.bfloat16)[..., None], block_base.shape + (sample_count,)
    )
    packed = jnp.concatenate(
        [
            kspace_samples,
            density[:, :, None],
            sample_frac,
            row_offsets.astype(jnp.bfloat16)[:, :, None],
            depth_base.astype(jnp.bfloat16)[:, :, None],
            corner_rows,
        ],
        axis=2,
    )
    tables = row_tables(grid_size, tile_here * slab) + (
        depth_table(grid_size), plane_table(grid_size),
    )
    even = frame_here % 2 == 0
    order = [jnp.where(even, last, 0), jnp.where(even, 0, last)]

    halves, received = [], []
    for place, frame in enumerate(order):
        own, other = gather_blocks(lax.dynamic_index_in_dim(packed, frame, 0, keepdims=False))
        corner = jnp.concatenate([own[:, -2:, 0], other[:, -2:, 0]], axis=0)
        corner = jnp.concatenate([frame[None].astype(jnp.int32), corner.reshape(-1).astype(jnp.int32)])
        half, small = frame_image(corner, own, other, tables, coil_maps, estimate, scale)
        halves.append(half)
        if place == 0:
            pairs = [(index, index ^ 1) for index in range(frame_count) if index ^ 1 < frame_count]
        else:
            pairs = [(index, index - 1) for index in range(2, frame_count, 2)]
            pairs += [(target, source) for source, target in pairs]
        received.append(lax.ppermute(small, "frame", pairs) if pairs else jnp.zeros_like(small))

    first = jnp.where(even, halves[1], halves[0])
    second = jnp.where(even, halves[0], halves[1])
    before = jnp.where(even, received[1], received[0]).astype(jnp.float32)
    after = jnp.where(even, received[0], received[1]).astype(jnp.float32)

    def psi(low, high):
        change = high - low
        return change / jnp.sqrt(
            change[0] * change[0] + change[1] * change[1] + EPS * EPS
        )[None]

    middle = psi(first, second)
    low = jnp.where(frame_here > 0, psi(before, first), 0.0)
    high = jnp.where(frame_here < frame_count - 1, psi(second, after), 0.0)
    return jnp.stack(
        [first - LAMBDA_TV * (low - middle), second - LAMBDA_TV * (middle - high)], axis=0
    )


def solution(mesh):
    in_specs = (
        P("frame", "tile", None, None),
        P("frame", "tile", None),
        P("frame", "tile", None, None),
        P("frame", "tile", None),
        P("frame", "tile", None),
        P("frame", "tile", None),
        P(None, None, "tile", None, None),
        P("frame", None, "tile", None, None),
    )
    out_specs = P("frame", None, "tile", None, None)
    return jax.shard_map(
        on_device, mesh=mesh, in_specs=in_specs, out_specs=out_specs, check_vma=False
    )
```

```python
import functools
import math

import jax
import jax.numpy as jnp
import numpy as np
from jax import lax
from jax.experimental import pallas as pl
from jax.experimental.pallas import tpu as pltpu
from jax.sharding import PartitionSpec as P

TAPS = 6
WIN = 8
YROWS = 8
META = 8
BETA = 13.9
EPS = 0.05
LAMBDA_TV = 0.3
TERMS = 40
UNROLL = 8
GROUPS = 8
LAST_REFS = 15
VMEM_LIMIT = 56 * 1024 * 1024


def kaiser_coefficients():
    quarter = BETA * BETA / 4.0
    terms = [quarter**power / math.factorial(power) ** 2 for power in range(TERMS)]
    total = math.fsum(terms)
    return [term / total for term in terms]


def kaiser(distance):
    coefficients = kaiser_coefficients()
    inside = jnp.maximum(1.0 - distance / 3.0 * (distance / 3.0), 0.0)
    value = jnp.full_like(inside, coefficients[-1])
    for coefficient in coefficients[-2::-1]:
        value = value * inside + coefficient
    return value


def dft_angles(grid_size):
    positions = np.arange(grid_size)
    return (positions[:, None] * positions[None, :] % grid_size) * (2.0 * math.pi / grid_size)


def depth_table(grid_size):
    angles = dft_angles(grid_size)
    return jnp.asarray(np.concatenate([np.cos(angles), np.sin(angles)], axis=0), jnp.bfloat16)


def plane_table(grid_size):
    angles = dft_angles(grid_size)
    cosine, sine = np.cos(angles), np.sin(angles)
    parts = np.stack([np.concatenate([cosine, -sine], 1), np.concatenate([sine, cosine], 1)])
    tiles = parts.reshape(2, grid_size // 8, 8, 2 * grid_size).swapaxes(0, 1)
    return jnp.asarray(tiles.reshape(2 * grid_size, 2 * grid_size), jnp.bfloat16)


def row_table(grid_size, tile_count):
    slab = grid_size // tile_count
    lanes = -(-(grid_size + WIN) // 128) * 128
    rows = np.arange(tile_count)[:, None, None] * slab + np.arange(YROWS)[:, None]
    angles = (rows * np.arange(lanes) % grid_size) * (2.0 * math.pi / grid_size)
    return jnp.asarray(np.stack([np.cos(angles), np.sin(angles)], axis=1), jnp.float32)


def shared_first():
    return lax.rem(lax.axis_index("frame"), 2) == 0


def pack_kernel(samples, density, fractions, shift, depth, corner, *packed):
    frames, blocks, _, count = samples.shape
    last = frames - 1
    for place, out in enumerate(packed):
        frame = jnp.where(shared_first(), last - place, place)
        rows = [
            density[frame].astype(jnp.float32)[:, None],
            fractions[frame].astype(jnp.float32),
            shift[frame].astype(jnp.float32)[:, None],
            depth[frame].astype(jnp.float32)[:, None],
        ]
        for block in range(blocks):
            ends = [
                jnp.full((1, count), corner[frame, block, axis], jnp.int32).astype(jnp.float32)
                for axis in range(2)
            ]
            parts = [samples[frame, block].astype(jnp.float32)] + [row[block] for row in rows] + ends
            out[block] = jnp.concatenate(parts, axis=0).astype(jnp.bfloat16)


def pack_blocks(samples, density, fractions, shift, depth, corner):
    frames, blocks, channels, count = samples.shape
    whole = pl.BlockSpec(memory_space=pltpu.VMEM)
    shape = jax.ShapeDtypeStruct((blocks, channels + META, count), jnp.bfloat16)
    return pl.pallas_call(
        pack_kernel,
        out_shape=(shape,) * frames,
        in_specs=[whole] * 5 + [pl.BlockSpec(memory_space=pltpu.SMEM)],
        out_specs=(whole,) * frames,
    )(samples, density, fractions, shift, depth, corner)


def frame_kernel(
    own, other, depth_dft, plane_dft, rows_hbm, maps_hbm, estimate_hbm, half, *rest, place, scale,
):
    half_small = rest[0] if len(rest) == LAST_REFS + 1 else None
    frame_body(
        own, other, depth_dft, plane_dft, rows_hbm, maps_hbm, estimate_hbm, half, half_small,
        *rest[-LAST_REFS:], place=place, scale=scale,
    )


def frame_body(
    own, other, depth_dft, plane_dft, rows_hbm, maps_hbm, estimate_hbm, half, half_small,
    cos_rows, sin_rows, corner_rows, corner, row_phases,
    grid_real, grid_imag, left, weights, weight_x, weight_y, maps, estimate, total, sems,
    *, place, scale,
):
    blocks = own.shape[0]
    samples = own.shape[2]
    unroll = len(left)
    coils, _, slab, grid_size, _ = maps.shape
    frame = jnp.where(shared_first(), estimate_hbm.shape[0] - 1 - place, place)
    copies = [
        pltpu.make_async_copy(maps_hbm, maps, sems.at[0]),
        pltpu.make_async_copy(estimate_hbm.at[frame], estimate, sems.at[1]),
    ]
    phases = pltpu.make_async_copy(rows_hbm.at[lax.axis_index("tile")], row_phases, sems.at[2])
    phases.start()
    for copy in copies:
        copy.start()
    for source, offset in ((own, 0), (other, blocks)):
        for block in range(blocks):
            ends = source[block].astype(jnp.float32)[2 * coils + META - 2 :]
            corner_rows[pl.ds(offset + block, 1), :] = (ends[:1] + grid_size * ends[1:]).astype(jnp.int32)
    corners = pltpu.make_async_copy(corner_rows, corner, sems.at[3])
    corners.start()
    phases.wait()
    for position in range(grid_size + WIN):
        at = slice(position, position + 1)
        cos_rows[position] = jnp.broadcast_to(row_phases[0, :, at], (YROWS, samples))
        sin_rows[position] = jnp.broadcast_to(row_phases[1, :, at], (YROWS, samples))

    table = depth_dft[...]
    taps = lax.broadcasted_iota(jnp.int32, (8, 2 * samples), 0).astype(jnp.float32)
    cells = lax.broadcasted_iota(jnp.int32, (grid_size, 2 * samples), 0).astype(jnp.bfloat16)
    clear_rows = grid_real[0].shape[1] // (blocks // unroll)

    def prepare(source, offset, cleared):
        def two(first):
            meta = jnp.concatenate(
                [source[first + part].astype(jnp.float32)[2 * coils :] for part in range(2)], axis=1
            )
            density, frac_x, frac_y, frac_z, shift, depth = (meta[row : row + 1] for row in range(6))
            tap_x = kaiser(taps - 2.0 - frac_x) * density
            lag = taps - shift
            tap_y = jnp.where((lag >= 0.0) & (lag < float(TAPS)), kaiser(lag - 2.0 - frac_y), 0.0)
            tap_z = kaiser(taps - 2.0 - frac_z).astype(jnp.bfloat16)
            cell = depth + taps
            cell = jnp.where(cell >= float(grid_size), cell - float(grid_size), cell)
            cell = cell.astype(jnp.bfloat16)
            spread = jnp.zeros((grid_size, 2 * samples), jnp.bfloat16)
            for tap in range(TAPS):
                spread = jnp.where(cells == cell[tap : tap + 1], tap_z[tap : tap + 1], spread)
            turned = jnp.dot(table, spread, preferred_element_type=jnp.float32).astype(jnp.bfloat16)
            real, imag = turned[:grid_size], turned[grid_size:]
            for part in range(2):
                at, here = offset + first + part, slice(part * samples, (part + 1) * samples)
                weight_x[at] = tap_x[:, here]
                weight_y[at] = tap_y[:, here]
                weights[at, :, :samples] = turned[:, here]
                weights[at, :grid_size, samples:] = -imag[:, here]
                weights[at, grid_size:, samples:] = real[:, here]

        def step(index, carry):
            for ref in cleared:
                at = pl.ds(pl.multiple_of(index * clear_rows, 8), clear_rows)
                ref[:, at, :] = jnp.zeros((ref.shape[0], clear_rows, grid_size), jnp.float32)
            for part in range(0, unroll, 2):
                two(index * unroll + part)
            return carry

        lax.fori_loop(0, blocks // unroll, step, 0)

    prepare(own, 0, grid_real)
    prepare(other, blocks, grid_imag)

    def build(source, offset, block, slot):
        first_row = corner[offset + block, 0] // grid_size
        payload = source[block].astype(jnp.float32)
        row_weights = weight_y[offset + block]
        plane_weights = weight_x[offset + block]
        turn_real = jnp.zeros((YROWS, samples), jnp.float32)
        turn_imag = jnp.zeros((YROWS, samples), jnp.float32)
        for row in range(WIN):
            weight = row_weights[row : row + 1]
            turn_real = turn_real + cos_rows[first_row + row] * weight
            turn_imag = turn_imag + sin_rows[first_row + row] * weight
        by_plane = []
        for tap in range(0, TAPS, 2):
            by_plane.append(jnp.concatenate(
                [jnp.broadcast_to(plane_weights[at : at + 1], (YROWS, samples)) for at in (tap, tap + 1)],
                axis=0,
            ).astype(jnp.bfloat16))
        for coil in range(coils):
            amp_real = payload[2 * coil : 2 * coil + 1]
            amp_imag = payload[2 * coil + 1 : 2 * coil + 2]
            parts = (
                amp_real * turn_real - amp_imag * turn_imag,
                amp_real * turn_imag + amp_imag * turn_real,
            )
            for part, value in enumerate(parts):
                twice = jnp.concatenate([value, value], axis=0).astype(jnp.bfloat16)
                for pair, weight in enumerate(by_plane):
                    left[slot][
                        pl.ds(coil * TAPS * YROWS + pair * 2 * YROWS, 2 * YROWS),
                        pl.ds(part * samples, samples),
                    ] = twice * weight

    def spread(offset, block, slot):
        first_plane = lax.rem(corner[offset + block, 0], grid_size)
        product = lax.dot_general(
            left[slot][...], weights[offset + block], (((1,), (1,)), ((), ())),
            preferred_element_type=jnp.float32,
        )
        rows = TAPS * YROWS
        per = grid_real[0].shape[0]
        for coil in range(coils):
            at = pl.ds(pl.multiple_of(first_plane * YROWS, YROWS), rows)
            part = product[coil * rows : (coil + 1) * rows]
            real, imag = grid_real[coil // per], grid_imag[coil // per]
            real[coil % per, at, :] = real[coil % per, at, :] + part[:, :grid_size]
            imag[coil % per, at, :] = imag[coil % per, at, :] + part[:, grid_size:]

    def spread_planes(source, offset):
        build(source, offset, 0, 0)

        def step(index, carry):
            block = index * unroll
            for part in range(unroll):
                later = jnp.minimum(block + part + 1, blocks - 1)
                build(source, offset, later, (part + 1) % unroll)
                spread(offset, block + part, part)
            return carry

        lax.fori_loop(0, blocks // unroll, step, 0)

    corners.wait()
    spread_planes(own, 0)
    spread_planes(other, blocks)

    wrap = (TAPS - 1) * YROWS
    top = grid_size * YROWS
    for ref in grid_real + grid_imag:
        ref[:, :wrap, :] = ref[:, :wrap, :] + ref[:, top : top + wrap, :]

    for copy in copies:
        copy.wait()

    columns = weights
    groups = len(grid_real)

    def coil_sums(index, carry):
        for place in range(groups):
            lanes = slice((place % 2) * grid_size, (place % 2 + 1) * grid_size)
            first = (place // 2) * YROWS
            for part, refs in enumerate((grid_real, grid_imag)):
                for start in range(0, grid_size, 16):
                    planes = refs[place][index, start * YROWS : (start + 16) * YROWS, :]
                    rows = jnp.swapaxes(planes.reshape(16, YROWS, grid_size), 0, 1)
                    at = slice(part * grid_size + start, part * grid_size + start + 16)
                    columns[first : first + YROWS, at, lanes] = rows.astype(jnp.bfloat16)
        for row in range(slab):
            images = [
                jnp.dot(
                    plane_dft[...], columns[pair * YROWS + row], preferred_element_type=jnp.float32
                )
                for pair in range(groups // 2)
            ]
            for tile in range(grid_size // 16):
                at = pl.ds(tile * 16, 16)
                sum_real, sum_imag = total[0, row, at], total[1, row, at]
                for place in range(groups):
                    coil = place * (coils // groups) + index
                    column = (place % 2) * grid_size
                    image = images[place // 2][tile * 32 : tile * 32 + 32, column : column + grid_size]
                    image_real = jnp.concatenate([image[:8], image[16:24]], axis=0)
                    image_imag = jnp.concatenate([image[8:16], image[24:]], axis=0)
                    map_real = maps[coil, 0, row, at].astype(jnp.float32)
                    map_imag = maps[coil, 1, row, at].astype(jnp.float32)
                    sum_real = sum_real + (map_real * image_real + map_imag * image_imag)
                    sum_imag = sum_imag + (map_real * image_imag - map_imag * image_real)
                total[0, row, at] = sum_real
                total[1, row, at] = sum_imag
        return carry

    total[...] = jnp.zeros_like(total)
    lax.fori_loop(0, coils // groups, coil_sums, 0)
    for part in range(2):
        for row in range(slab):
            value = estimate[part, row] + scale * total[part, row]
            half[part, row] = value
            if half_small is not None:
                half_small[part, row] = value.astype(jnp.bfloat16)


def frame_image(own, other, tables, coil_maps, estimate, scale, place, shared):
    blocks, _, samples = own.shape
    coils, _, slab, grid_size, _ = coil_maps.shape
    shape = (2, slab, grid_size, grid_size)
    whole = pl.BlockSpec(memory_space=pltpu.VMEM)
    away = pl.BlockSpec(memory_space=pl.ANY)
    unroll = math.gcd(blocks, UNROLL)
    grid_shape = (coils // GROUPS, (grid_size + WIN) * YROWS, grid_size)
    outs = (jnp.float32, jnp.bfloat16)[: 2 if shared else 1]
    return pl.pallas_call(
        functools.partial(frame_kernel, place=place, scale=scale),
        out_shape=tuple(jax.ShapeDtypeStruct(shape, kind) for kind in outs),
        in_specs=[whole] * 4 + [away] * 3,
        out_specs=(whole,) * len(outs),
        scratch_shapes=[
            pltpu.VMEM((grid_size + WIN, YROWS, samples), jnp.float32),
            pltpu.VMEM((grid_size + WIN, YROWS, samples), jnp.float32),
            pltpu.VMEM((2 * blocks, samples), jnp.int32),
            pltpu.SMEM((2 * blocks, samples), jnp.int32),
            pltpu.VMEM(tables[2].shape[1:], jnp.float32),
            [pltpu.VMEM(grid_shape, jnp.float32)] * GROUPS,
            [pltpu.VMEM(grid_shape, jnp.float32)] * GROUPS,
            [pltpu.VMEM((coils * TAPS * YROWS, 2 * samples), jnp.bfloat16)] * unroll,
            pltpu.VMEM((2 * blocks, 2 * grid_size, 2 * samples), jnp.bfloat16),
            pltpu.VMEM((2 * blocks, 8, samples), jnp.float32),
            pltpu.VMEM((2 * blocks, 8, samples), jnp.float32),
            pltpu.VMEM(coil_maps.shape, jnp.bfloat16),
            pltpu.VMEM(shape, jnp.float32),
            pltpu.VMEM(shape, jnp.float32),
            pltpu.SemaphoreType.DMA((4,)),
        ],
        compiler_params=pltpu.CompilerParams(vmem_limit_bytes=VMEM_LIMIT),
        cost_estimate=pl.CostEstimate(
            flops=2 * 2 * blocks * TAPS * coils * YROWS * 4 * samples * grid_size,
            bytes_accessed=coil_maps.size * 2,
            transcendentals=0,
        ),
    )(own, other, *tables, coil_maps, estimate)


def step_kernel(first, second, beside_first, beside_second, out):
    index, count = lax.axis_index("frame"), lax.axis_size("frame")
    even = shared_first()

    def slope(low, high):
        change = high - low
        return change * lax.rsqrt(change[0] * change[0] + change[1] * change[1] + EPS * EPS)[None]

    values = first[...], second[...]
    pull = slope(values[0], values[1])
    has = (
        jnp.where(even, index + 1 < count, True),
        jnp.where(even, index > 0, index + 1 < count),
    )
    place = jnp.where(even, 1, 0)
    for value, inner, beside, there, at in (
        (values[0], pull, beside_first, has[0], place),
        (values[1], -pull, beside_second, has[1], 1 - place),
    ):
        if beside is not None:
            outer = slope(value, beside[...].astype(jnp.float32))
            inner = inner + jnp.where(there, outer, 0.0)
        out[at] = value + LAMBDA_TV * inner


def tv_step(halves, received):
    parts, slab, grid_size, _ = halves[0].shape
    block = pl.BlockSpec((parts, 1, grid_size, grid_size), lambda row: (0, row, 0, 0))
    given = [value for value in received if value is not None]

    def kernel(first, second, *rest):
        step_kernel(first, second, rest[0], rest[1] if len(given) > 1 else None, rest[-1])

    return pl.pallas_call(
        kernel,
        grid=(slab,),
        out_shape=jax.ShapeDtypeStruct((2,) + halves[0].shape, jnp.float32),
        in_specs=[block] * (2 + len(given)),
        out_specs=pl.BlockSpec((2, parts, 1, grid_size, grid_size), lambda row: (0, 0, row, 0, 0)),
    )(*halves, *given)


def swap(values, axis, bit):
    count = lax.axis_size(axis)
    return lax.ppermute(values, axis, [(index, index ^ bit) for index in range(count)])


def gather_blocks(packed):
    count = lax.axis_size("tile")
    held = packed[None]
    bits = [1 << place for place in range(1, count.bit_length() - 1)]
    for bit in reversed(bits):
        held = jnp.concatenate([held, swap(held, "tile", bit)], axis=0)
    held = held.reshape((-1,) + packed.shape[1:])
    return held, swap(held, "tile", 1)


def on_device(
    kspace_samples, density, sample_frac, row_offsets, depth_base, block_base, coil_maps, estimate
):
    tile_count = lax.axis_size("tile")
    frame_count = lax.axis_size("frame")
    frames_local, blocks_local, channels, sample_count = kspace_samples.shape
    grid_size = coil_maps.shape[3]
    scale = 1.0 / (8.0 * math.sqrt(blocks_local * tile_count * sample_count))

    packed = pack_blocks(
        kspace_samples, density, sample_frac, row_offsets, depth_base, block_base
    )
    tables = depth_table(grid_size), plane_table(grid_size), row_table(grid_size, tile_count)
    pairs = [
        [(index, index ^ 1) for index in range(frame_count) if index ^ 1 < frame_count],
        [(index, index - 1) for index in range(2, frame_count, 2)],
    ]
    pairs[1] += [(target, source) for source, target in pairs[1]]
    halves, received = [], []
    for place in range(2):
        own, other = gather_blocks(packed[place])
        half, *small = frame_image(
            own, other, tables, coil_maps, estimate, scale, place, bool(pairs[place])
        )
        halves.append(half)
        received.append(lax.ppermute(small[0], "frame", pairs[place]) if small else None)
    return tv_step(halves, received)


def solution(mesh):
    in_specs = (
        P("frame", "tile", None, None),
        P("frame", "tile", None),
        P("frame", "tile", None, None),
        P("frame", "tile", None),
        P("frame", "tile", None),
        P("frame", "tile", None),
        P(None, None, "tile", None, None),
        P("frame", None, "tile", None, None),
    )
    out_specs = P("frame", None, "tile", None, None)
    return jax.shard_map(
        on_device, mesh=mesh, in_specs=in_specs, out_specs=out_specs, check_vma=False
    )
```

```python
import functools
import math

import jax
import jax.numpy as jnp
import numpy as np
from jax import lax
from jax.experimental import pallas as pl
from jax.experimental.pallas import tpu as pltpu
from jax.sharding import PartitionSpec as P

TAPS = 6
WIN = 8
YROWS = 8
META = 8
BETA = 13.9
EPS = 0.05
LAMBDA_TV = 0.3
TERMS = 40
UNROLL = 8
GROUPS = 16
LAST_REFS = 16
VMEM_LIMIT = 52 * 1024 * 1024


def kaiser_coefficients():
    quarter = BETA * BETA / 4.0
    terms = [quarter**power / math.factorial(power) ** 2 for power in range(TERMS)]
    total = math.fsum(terms)
    return [term / total for term in terms]


def kaiser(distance):
    coefficients = kaiser_coefficients()
    inside = jnp.maximum(1.0 - distance / 3.0 * (distance / 3.0), 0.0)
    value = jnp.full_like(inside, coefficients[-1])
    for coefficient in coefficients[-2::-1]:
        value = value * inside + coefficient
    return value


def dft_angles(grid_size):
    positions = np.arange(grid_size)
    return (positions[:, None] * positions[None, :] % grid_size) * (2.0 * math.pi / grid_size)


def plane_table(grid_size):
    angles = dft_angles(grid_size)
    cosine, sine = np.cos(angles), np.sin(angles)
    parts = np.stack([np.concatenate([cosine, -sine], 1), np.concatenate([sine, cosine], 1)])
    tiles = parts.reshape(2, grid_size // 8, 8, 2 * grid_size).swapaxes(0, 1)
    return jnp.asarray(tiles.reshape(2 * grid_size, 2 * grid_size), jnp.bfloat16)


def shared_first():
    return lax.rem(lax.axis_index("frame"), 2) == 0


def pack_kernel(samples, density, fractions, shift, depth, corner, *packed):
    frames, blocks, _, count = samples.shape
    last = frames - 1
    for place, out in enumerate(packed):
        frame = jnp.where(shared_first(), last - place, place)
        rows = [
            density[frame].astype(jnp.float32)[:, None],
            jnp.swapaxes(fractions[frame].astype(jnp.float32), 0, 1),
            shift[frame].astype(jnp.float32)[:, None],
            depth[frame].astype(jnp.float32)[:, None],
        ]
        for block in range(blocks):
            ends = [
                jnp.full((1, count), corner[frame, axis, block], jnp.int32).astype(jnp.float32)
                for axis in range(2)
            ]
            parts = [samples[frame, block].astype(jnp.float32)] + [row[block] for row in rows] + ends
            out[block] = jnp.concatenate(parts, axis=0).astype(jnp.bfloat16)


def pack_blocks(samples, density, fractions, shift, depth, corner):
    frames, blocks, channels, count = samples.shape
    whole = pl.BlockSpec(memory_space=pltpu.VMEM)
    shape = jax.ShapeDtypeStruct((blocks, channels + META, count), jnp.bfloat16)
    return pl.pallas_call(
        pack_kernel,
        out_shape=(shape,) * frames,
        in_specs=[whole] * 5 + [pl.BlockSpec(memory_space=pltpu.SMEM)],
        out_specs=(whole,) * frames,
    )(samples, density, jnp.swapaxes(fractions, 1, 2), shift, depth, jnp.swapaxes(corner, 1, 2))


def frame_kernel(
    own, other, plane_hbm, maps_hbm, estimate_hbm, half, *rest, place, scale,
):
    half_small = rest[0] if len(rest) == LAST_REFS + 1 else None
    frame_body(
        own, other, plane_hbm, maps_hbm, estimate_hbm, half, half_small,
        *rest[-LAST_REFS:], place=place, scale=scale,
    )


def frame_body(
    own, other, plane_hbm, maps_hbm, estimate_hbm, half, half_small,
    depth_dft, plane_dft, cos_rows, sin_rows, corner_rows, corner,
    grid_real, grid_imag, left, weights, weight_x, weight_y, maps, estimate, total, sems,
    *, place, scale,
):
    blocks = own.shape[0]
    samples = own.shape[2]
    unroll = len(left)
    coils, _, slab, grid_size, _ = maps.shape
    frame = jnp.where(shared_first(), estimate_hbm.shape[0] - 1 - place, place)
    copies = [
        pltpu.make_async_copy(maps_hbm, maps, sems.at[0]),
        pltpu.make_async_copy(estimate_hbm.at[frame], estimate, sems.at[1]),
    ]
    planes = pltpu.make_async_copy(plane_hbm, plane_dft, sems.at[2])
    planes.start()
    for copy in copies:
        copy.start()
    for source, offset in ((own, 0), (other, blocks)):
        for block in range(blocks):
            ends = source[block].astype(jnp.float32)[2 * coils + META - 2 :]
            corner_rows[pl.ds(offset + block, 1), :] = (ends[:1] + grid_size * ends[1:]).astype(jnp.int32)
    corners = pltpu.make_async_copy(corner_rows, corner, sems.at[3])
    corners.start()
    lanes = -(-(grid_size + WIN) // 128) * 128
    position = lax.broadcasted_iota(jnp.int32, (YROWS, lanes), 1)
    image_y = lax.axis_index("tile") * slab + lax.broadcasted_iota(jnp.int32, (YROWS, lanes), 0)
    angles = lax.rem(position * image_y, grid_size).astype(jnp.float32) * (2.0 * math.pi / grid_size)
    for table, phases in ((cos_rows, jnp.cos(angles)), (sin_rows, jnp.sin(angles))):
        for k in range(grid_size + WIN):
            table[k] = jnp.broadcast_to(phases[:, k : k + 1], (YROWS, samples))
    planes.wait()
    tiles = plane_dft[:, :grid_size].astype(jnp.float32).reshape(grid_size // 8, 2, 8, grid_size)
    for part in range(2):
        at = slice(part * grid_size, (part + 1) * grid_size)
        depth_dft[at, :] = tiles[:, part].reshape(grid_size, grid_size).astype(jnp.bfloat16)

    table = depth_dft[...]
    taps = lax.broadcasted_iota(jnp.int32, (8, 2 * samples), 0).astype(jnp.float32)
    cells = lax.broadcasted_iota(jnp.int32, (grid_size, 2 * samples), 0).astype(jnp.bfloat16)
    clear_rows = grid_real[0].shape[1] // (blocks // unroll)

    def prepare(source, offset, cleared):
        def two(first):
            meta = jnp.concatenate(
                [source[first + part].astype(jnp.float32)[2 * coils :] for part in range(2)], axis=1
            )
            density, frac_x, frac_y, frac_z, shift, depth = (meta[row : row + 1] for row in range(6))
            tap_x = kaiser(taps - 2.0 - frac_x) * density
            lag = taps - shift
            tap_y = jnp.where((lag >= 0.0) & (lag < float(TAPS)), kaiser(lag - 2.0 - frac_y), 0.0)
            tap_z = kaiser(taps - 2.0 - frac_z).astype(jnp.bfloat16)
            cell = depth + taps
            cell = jnp.where(cell >= float(grid_size), cell - float(grid_size), cell)
            cell = cell.astype(jnp.bfloat16)
            spread = jnp.zeros((grid_size, 2 * samples), jnp.bfloat16)
            for tap in range(TAPS):
                spread = jnp.where(cells == cell[tap : tap + 1], tap_z[tap : tap + 1], spread)
            turned = jnp.dot(table, spread, preferred_element_type=jnp.float32).astype(jnp.bfloat16)
            real, imag = turned[:grid_size], turned[grid_size:]
            for part in range(2):
                at, here = offset + first + part, slice(part * samples, (part + 1) * samples)
                weight_x[at] = tap_x[:, here]
                weight_y[at] = tap_y[:, here]
                weights[at, :, :samples] = turned[:, here]
                weights[at, :grid_size, samples:] = -imag[:, here]
                weights[at, grid_size:, samples:] = real[:, here]

        def step(index, carry):
            for ref in cleared:
                at = pl.ds(pl.multiple_of(index * clear_rows, 8), clear_rows)
                ref[:, at, :] = jnp.zeros((ref.shape[0], clear_rows, grid_size), jnp.float32)
            for part in range(0, unroll, 2):
                two(index * unroll + part)
            return carry

        lax.fori_loop(0, blocks // unroll, step, 0)

    prepare(own, 0, grid_real)
    prepare(other, blocks, grid_imag)

    def build(source, offset, block, slot):
        first_row = corner[offset + block, 0] // grid_size
        payload = source[block].astype(jnp.float32)
        row_weights = weight_y[offset + block]
        plane_weights = weight_x[offset + block]
        turn_real = jnp.zeros((YROWS, samples), jnp.float32)
        turn_imag = jnp.zeros((YROWS, samples), jnp.float32)
        for row in range(WIN):
            weight = row_weights[row : row + 1]
            turn_real = turn_real + cos_rows[first_row + row] * weight
            turn_imag = turn_imag + sin_rows[first_row + row] * weight
        by_plane = []
        for tap in range(0, TAPS, 2):
            by_plane.append(jnp.concatenate(
                [jnp.broadcast_to(plane_weights[at : at + 1], (YROWS, samples)) for at in (tap, tap + 1)],
                axis=0,
            ).astype(jnp.bfloat16))
        for coil in range(coils):
            amp_real = payload[2 * coil : 2 * coil + 1]
            amp_imag = payload[2 * coil + 1 : 2 * coil + 2]
            parts = (
                amp_real * turn_real - amp_imag * turn_imag,
                amp_real * turn_imag + amp_imag * turn_real,
            )
            for part, value in enumerate(parts):
                twice = jnp.concatenate([value, value], axis=0).astype(jnp.bfloat16)
                for pair, weight in enumerate(by_plane):
                    left[slot][
                        pl.ds(coil * TAPS * YROWS + pair * 2 * YROWS, 2 * YROWS),
                        pl.ds(part * samples, samples),
                    ] = twice * weight

    def spread(offset, block, slot):
        first_plane = lax.rem(corner[offset + block, 0], grid_size)
        product = lax.dot_general(
            left[slot][...], weights[offset + block], (((1,), (1,)), ((), ())),
            preferred_element_type=jnp.float32,
        )
        rows = TAPS * YROWS
        per = grid_real[0].shape[0]
        for coil in range(coils):
            at = pl.ds(pl.multiple_of(first_plane * YROWS, YROWS), rows)
            part = product[coil * rows : (coil + 1) * rows]
            real, imag = grid_real[coil // per], grid_imag[coil // per]
            real[coil % per, at, :] = real[coil % per, at, :] + part[:, :grid_size]
            imag[coil % per, at, :] = imag[coil % per, at, :] + part[:, grid_size:]

    def spread_planes(source, offset):
        build(source, offset, 0, 0)

        def step(index, carry):
            block = index * unroll
            for part in range(unroll):
                later = jnp.minimum(block + part + 1, blocks - 1)
                build(source, offset, later, (part + 1) % unroll)
                spread(offset, block + part, part)
            return carry

        lax.fori_loop(0, blocks // unroll, step, 0)

    corners.wait()
    spread_planes(own, 0)
    spread_planes(other, blocks)

    wrap = (TAPS - 1) * YROWS
    top = grid_size * YROWS
    for ref in grid_real + grid_imag:
        ref[:, :wrap, :] = ref[:, :wrap, :] + ref[:, top : top + wrap, :]

    for copy in copies:
        copy.wait()

    columns = weights
    pairs = coils // 2
    per = grid_real[0].shape[0]

    def transpose(step, carry):
        start = step * 16
        for coil in range(coils):
            lanes = slice((coil % 2) * grid_size, (coil % 2 + 1) * grid_size)
            for part, refs in enumerate((grid_real, grid_imag)):
                at = pl.ds(pl.multiple_of(start * YROWS, 16 * YROWS), 16 * YROWS)
                planes = refs[coil // per][coil % per, at, :].reshape(16, YROWS, grid_size)
                rows = jnp.swapaxes(planes, 0, 1).astype(jnp.bfloat16)
                at = pl.ds(pl.multiple_of(part * grid_size + start, 16), 16)
                for row in range(slab):
                    columns[row * pairs + coil // 2, at, lanes] = rows[row]
        return carry

    lax.fori_loop(0, grid_size // 16, transpose, 0)

    def image_row(row, carry):
        for quad in range(coils // 4):
            images = [
                jnp.dot(
                    plane_dft[...], columns[row * pairs + pair], preferred_element_type=jnp.float32
                )
                for pair in (2 * quad, 2 * quad + 1)
            ]
            for tile in range(grid_size // 16):
                at = pl.ds(tile * 16, 16)
                sums = [[], []]
                for place in range(4):
                    coil = 4 * quad + place
                    column = (place % 2) * grid_size
                    image = images[place // 2][tile * 32 : tile * 32 + 32, column : column + grid_size]
                    image_real = jnp.concatenate([image[:8], image[16:24]], axis=0)
                    image_imag = jnp.concatenate([image[8:16], image[24:]], axis=0)
                    map_real = maps[coil, 0, row, at].astype(jnp.float32)
                    map_imag = maps[coil, 1, row, at].astype(jnp.float32)
                    sums[0].append(map_real * image_real + map_imag * image_imag)
                    sums[1].append(map_real * image_imag - map_imag * image_real)
                for part in range(2):
                    value = (sums[part][0] + sums[part][1]) + (sums[part][2] + sums[part][3])
                    if quad > 0:
                        value = value + total[part, at]
                    if quad < coils // 4 - 1:
                        total[part, at] = value
                    else:
                        value = estimate[part, row, at] + scale * value
                        half[part, row, at] = value
                        if half_small is not None:
                            half_small[part, row, at] = value.astype(jnp.bfloat16)
        return carry

    lax.fori_loop(0, slab, image_row, 0)


def frame_image(own, other, plane_dft, coil_maps, estimate, scale, place, shared):
    blocks, _, samples = own.shape
    coils, _, slab, grid_size, _ = coil_maps.shape
    shape = (2, slab, grid_size, grid_size)
    whole = pl.BlockSpec(memory_space=pltpu.VMEM)
    away = pl.BlockSpec(memory_space=pltpu.HBM)
    unroll = math.gcd(blocks, UNROLL)
    grid_shape = (coils // math.gcd(coils, GROUPS), (grid_size + WIN) * YROWS, grid_size)
    outs = (jnp.float32, jnp.bfloat16)[: 2 if shared else 1]
    return pl.pallas_call(
        functools.partial(frame_kernel, place=place, scale=scale),
        out_shape=tuple(jax.ShapeDtypeStruct(shape, kind) for kind in outs),
        in_specs=[whole] * 2 + [away] * 3,
        out_specs=(whole,) * len(outs),
        scratch_shapes=[
            pltpu.VMEM((2 * grid_size, grid_size), jnp.bfloat16),
            pltpu.VMEM(plane_dft.shape, jnp.bfloat16),
            pltpu.VMEM((grid_size + WIN, YROWS, samples), jnp.float32),
            pltpu.VMEM((grid_size + WIN, YROWS, samples), jnp.float32),
            pltpu.VMEM((2 * blocks, samples), jnp.int32),
            pltpu.SMEM((2 * blocks, samples), jnp.int32),
            [pltpu.VMEM(grid_shape, jnp.float32)] * math.gcd(coils, GROUPS),
            [pltpu.VMEM(grid_shape, jnp.float32)] * math.gcd(coils, GROUPS),
            [pltpu.VMEM((coils * TAPS * YROWS, 2 * samples), jnp.bfloat16)] * unroll,
            pltpu.VMEM((2 * blocks, 2 * grid_size, 2 * samples), jnp.bfloat16),
            pltpu.VMEM((2 * blocks, 8, samples), jnp.float32),
            pltpu.VMEM((2 * blocks, 8, samples), jnp.float32),
            pltpu.VMEM(coil_maps.shape, jnp.bfloat16),
            pltpu.VMEM(shape, jnp.float32),
            pltpu.VMEM((2, grid_size, grid_size), jnp.float32),
            pltpu.SemaphoreType.DMA((4,)),
        ],
        compiler_params=pltpu.CompilerParams(vmem_limit_bytes=VMEM_LIMIT),
        cost_estimate=pl.CostEstimate(
            flops=2 * 2 * blocks * TAPS * coils * YROWS * 4 * samples * grid_size,
            bytes_accessed=coil_maps.size * 2,
            transcendentals=0,
        ),
    )(own, other, plane_dft, coil_maps, estimate)


def step_kernel(first, second, *rest):
    *besides, out_hbm, out, sems = rest
    index, count = lax.axis_index("frame"), lax.axis_size("frame")
    even = shared_first()
    place = jnp.where(even, 1, 0)
    there = (
        jnp.where(even, index + 1 < count, True),
        jnp.where(even, index > 0, index + 1 < count),
    )

    def slope(low, high):
        change = high - low
        return change * lax.rsqrt(change[0] * change[0] + change[1] * change[1] + EPS * EPS)[None]

    copies = []
    for row in range(out.shape[2]):
        values = first[:, row], second[:, row]
        pull = slope(values[0], values[1])
        pulls = [pull, -pull]
        for side, beside in enumerate(besides):
            outer = slope(values[side], beside[:, row].astype(jnp.float32))
            pulls[side] = pulls[side] + jnp.where(there[side], outer, 0.0)
        for side, at in enumerate((place, 1 - place)):
            out[side, :, row] = values[side] + LAMBDA_TV * pulls[side]
            copies.append(pltpu.make_async_copy(
                out.at[side, :, row], out_hbm.at[at, :, row], sems.at[side, row]
            ))
            copies[-1].start()
    for copy in copies:
        copy.wait()


def tv_step(halves, received):
    given = [value for value in received if value is not None]
    whole = pl.BlockSpec(memory_space=pltpu.VMEM)
    shape = (2,) + halves[0].shape
    return pl.pallas_call(
        step_kernel,
        out_shape=jax.ShapeDtypeStruct(shape, jnp.float32),
        in_specs=[whole] * (2 + len(given)),
        out_specs=pl.BlockSpec(memory_space=pltpu.HBM),
        scratch_shapes=[
            pltpu.VMEM(shape, jnp.float32),
            pltpu.SemaphoreType.DMA((2, shape[2])),
        ],
        compiler_params=pltpu.CompilerParams(vmem_limit_bytes=VMEM_LIMIT // 4),
    )(*halves, *given)


def swap(values, axis, bit):
    count = lax.axis_size(axis)
    return lax.ppermute(values, axis, [(index, index ^ bit) for index in range(count)])


def join_halves(held):
    return jnp.concatenate([held, swap(held, "tile", lax.axis_size("tile") // 2)], axis=0)


def chips(held):
    shifts = range(2, lax.axis_size("tile") // 2, 2)
    return [held] + [swap(held, "tile", shift) for shift in shifts]


def on_device(
    kspace_samples, density, sample_frac, row_offsets, depth_base, block_base, coil_maps, estimate
):
    tile_count = lax.axis_size("tile")
    frame_count = lax.axis_size("frame")
    frames_local, blocks_local, channels, sample_count = kspace_samples.shape
    grid_size = coil_maps.shape[3]
    scale = 1.0 / (8.0 * math.sqrt(blocks_local * tile_count * sample_count))

    packed = pack_blocks(
        kspace_samples, density, sample_frac, row_offsets, depth_base, block_base
    )
    plane_dft = plane_table(grid_size)
    pairs = [
        [(index, index ^ 1) for index in range(frame_count) if index ^ 1 < frame_count],
        [(index, index - 1) for index in range(2, frame_count, 2)],
    ]
    pairs[1] += [(target, source) for source, target in pairs[1]]
    shared, rest = packed
    shared = join_halves(shared)
    rest, shared = lax.optimization_barrier((rest, shared))
    rest = join_halves(rest)
    shared = chips(shared)
    rest, *shared = lax.optimization_barrier((rest, *shared))
    held = [jnp.concatenate(shared, axis=0), chips(rest)]
    halves, received = [], []
    for place in range(2):
        if place == 1:
            (*pieces, halves[0]) = lax.optimization_barrier((*held[1], halves[0]))
            held[1] = jnp.concatenate(pieces, axis=0)
        half, *small = frame_image(
            held[place], swap(held[place], "tile", 1), plane_dft, coil_maps, estimate, scale, place,
            bool(pairs[place]),
        )
        halves.append(half)
        received.append(lax.ppermute(small[0], "frame", pairs[place]) if small else None)
    return tv_step(halves, received)


def solution(mesh):
    in_specs = (
        P("frame", "tile", None, None),
        P("frame", "tile", None),
        P("frame", "tile", None, None),
        P("frame", "tile", None),
        P("frame", "tile", None),
        P("frame", "tile", None),
        P(None, None, "tile", None, None),
        P("frame", None, "tile", None, None),
    )
    out_specs = P("frame", None, "tile", None, None)
    return jax.shard_map(
        on_device, mesh=mesh, in_specs=in_specs, out_specs=out_specs, check_vma=False
    )
```

```python
import functools
import math

import jax
import jax.numpy as jnp
import numpy as np
from jax import lax
from jax.experimental import pallas as pl
from jax.experimental.pallas import tpu as pltpu
from jax.sharding import PartitionSpec as P

TAPS = 6
WIN = 8
YROWS = 8
META = 8
BETA = 13.9
EPS = 0.05
LAMBDA_TV = 0.3
TERMS = 40
UNROLL = 16
AHEAD = 16
GROUPS = 16
LAST_REFS = 16
VMEM_LIMIT = 52 * 1024 * 1024


def kaiser_coefficients():
    quarter = BETA * BETA / 4.0
    terms = [quarter**power / math.factorial(power) ** 2 for power in range(TERMS)]
    total = math.fsum(terms)
    return [term / total for term in terms]


def kaiser(distance):
    coefficients = kaiser_coefficients()
    inside = jnp.maximum(1.0 - distance / 3.0 * (distance / 3.0), 0.0)
    value = jnp.full_like(inside, coefficients[-1])
    for coefficient in coefficients[-2::-1]:
        value = value * inside + coefficient
    return value


def dft_angles(grid_size):
    positions = np.arange(grid_size)
    return (positions[:, None] * positions[None, :] % grid_size) * (2.0 * math.pi / grid_size)


def plane_table(grid_size):
    angles = dft_angles(grid_size)
    cosine, sine = np.cos(angles), np.sin(angles)
    parts = np.stack([np.concatenate([cosine, -sine], 1), np.concatenate([sine, cosine], 1)])
    tiles = parts.reshape(2, grid_size // 8, 8, 2 * grid_size).swapaxes(0, 1)
    return jnp.asarray(tiles.reshape(2 * grid_size, 2 * grid_size), jnp.bfloat16)


def shared_first():
    return lax.rem(lax.axis_index("frame"), 2) == 0


def pack_kernel(samples, density, fractions, shift, depth, corner, packed):
    frames, blocks, _, count = samples.shape
    last = frames - 1
    for place in range(frames):
        frame = jnp.where(shared_first(), last - place, place)
        rows = [
            density[frame].astype(jnp.float32)[:, None],
            jnp.swapaxes(fractions[frame].astype(jnp.float32), 0, 1),
            shift[frame].astype(jnp.float32)[:, None],
            depth[frame].astype(jnp.float32)[:, None],
        ]
        for block in range(blocks):
            ends = [
                jnp.full((1, count), corner[frame, axis, block], jnp.int32).astype(jnp.float32)
                for axis in range(2)
            ]
            parts = [samples[frame, block].astype(jnp.float32)] + [row[block] for row in rows] + ends
            packed[place, block] = jnp.concatenate(parts, axis=0).astype(jnp.bfloat16)


def pack_blocks(samples, density, fractions, shift, depth, corner):
    frames, blocks, channels, count = samples.shape
    whole = pl.BlockSpec(memory_space=pltpu.VMEM)
    return pl.pallas_call(
        pack_kernel,
        out_shape=jax.ShapeDtypeStruct((frames, blocks, channels + META, count), jnp.bfloat16),
        in_specs=[whole] * 5 + [pl.BlockSpec(memory_space=pltpu.SMEM)],
        out_specs=whole,
    )(samples, density, jnp.swapaxes(fractions, 1, 2), shift, depth, jnp.swapaxes(corner, 1, 2))


def frame_kernel(
    own, other, plane_hbm, maps_hbm, estimate_hbm, half, *rest, place, scale,
):
    half_small = rest[0] if len(rest) == LAST_REFS + 1 else None
    frame_body(
        own, other, plane_hbm, maps_hbm, estimate_hbm, half, half_small,
        *rest[-LAST_REFS:], place=place, scale=scale,
    )


def frame_body(
    own, other, plane_hbm, maps_hbm, estimate_hbm, half, half_small,
    depth_dft, plane_dft, cos_rows, sin_rows, corner_rows, corner,
    grid_real, grid_imag, left, weights, weight_x, weight_y, maps, estimate, total, sems,
    *, place, scale,
):
    blocks = own.shape[0]
    samples = own.shape[2]
    unroll = len(left)
    coils, _, slab, grid_size, _ = maps.shape
    frame = jnp.where(shared_first(), estimate_hbm.shape[0] - 1 - place, place)
    copies = [
        pltpu.make_async_copy(maps_hbm, maps, sems.at[0]),
        pltpu.make_async_copy(estimate_hbm.at[frame], estimate, sems.at[1]),
    ]
    planes = pltpu.make_async_copy(plane_hbm, plane_dft, sems.at[2])
    planes.start()
    for copy in copies:
        copy.start()
    for source, offset in ((own, 0), (other, blocks)):
        for block in range(blocks):
            ends = source[block].astype(jnp.float32)[2 * coils + META - 2 :]
            corner_rows[pl.ds(offset + block, 1), :] = (ends[:1] + grid_size * ends[1:]).astype(jnp.int32)
    corners = pltpu.make_async_copy(corner_rows, corner, sems.at[3])
    corners.start()
    lanes = -(-(grid_size + WIN) // 128) * 128
    position = lax.broadcasted_iota(jnp.int32, (YROWS, lanes), 1)
    image_y = lax.axis_index("tile") * slab + lax.broadcasted_iota(jnp.int32, (YROWS, lanes), 0)
    angles = lax.rem(position * image_y, grid_size).astype(jnp.float32) * (2.0 * math.pi / grid_size)
    phases = jnp.cos(angles), jnp.sin(angles)
    stride = 16
    turn, *chain = (
        tuple(jnp.broadcast_to(phase[:, k : k + 1], (YROWS, samples)) for phase in phases)
        for k in (stride, *range(stride))
    )
    for k in range(grid_size + WIN):
        real, imag = chain[k % stride]
        cos_rows[k], sin_rows[k] = real, imag
        chain[k % stride] = real * turn[0] - imag * turn[1], real * turn[1] + imag * turn[0]
    planes.wait()
    tiles = plane_dft[:, :grid_size].astype(jnp.float32).reshape(grid_size // 8, 2, 8, grid_size)
    for part in range(2):
        at = slice(part * grid_size, (part + 1) * grid_size)
        depth_dft[at, :] = tiles[:, part].reshape(grid_size, grid_size).astype(jnp.bfloat16)

    table = depth_dft[...]
    taps = lax.broadcasted_iota(jnp.int32, (8, 2 * samples), 0).astype(jnp.float32)
    cells = lax.broadcasted_iota(jnp.int32, (grid_size, 2 * samples), 0).astype(jnp.bfloat16)
    ahead = math.gcd(blocks, AHEAD)
    clear_rows = grid_real[0].shape[1] // (blocks // ahead)

    def prepare(source, offset, cleared):
        def two(first):
            meta = jnp.concatenate(
                [source[first + part].astype(jnp.float32)[2 * coils :] for part in range(2)], axis=1
            )
            density, frac_x, frac_y, frac_z, shift, depth = (meta[row : row + 1] for row in range(6))
            tap_x = kaiser(taps - 2.0 - frac_x) * density
            lag = taps - shift
            tap_y = jnp.where((lag >= 0.0) & (lag < float(TAPS)), kaiser(lag - 2.0 - frac_y), 0.0)
            tap_z = kaiser(taps - 2.0 - frac_z).astype(jnp.bfloat16)
            cell = depth + taps
            cell = jnp.where(cell >= float(grid_size), cell - float(grid_size), cell)
            cell = cell.astype(jnp.bfloat16)
            spread = jnp.zeros((grid_size, 2 * samples), jnp.bfloat16)
            for tap in range(TAPS):
                spread = jnp.where(cells == cell[tap : tap + 1], tap_z[tap : tap + 1], spread)
            turned = jnp.dot(table, spread, preferred_element_type=jnp.float32).astype(jnp.bfloat16)
            real, imag = turned[:grid_size], turned[grid_size:]
            for part in range(2):
                at, here = offset + first + part, slice(part * samples, (part + 1) * samples)
                weight_x[at] = tap_x[:, here]
                weight_y[at] = tap_y[:, here]
                weights[at, :, :samples] = turned[:, here]
                weights[at, :grid_size, samples:] = -imag[:, here]
                weights[at, grid_size:, samples:] = real[:, here]

        def step(index, carry):
            for ref in cleared:
                at = pl.ds(pl.multiple_of(index * clear_rows, 8), clear_rows)
                ref[:, at, :] = jnp.zeros((ref.shape[0], clear_rows, grid_size), jnp.float32)
            for part in range(0, ahead, 2):
                two(index * ahead + part)
            return carry

        lax.fori_loop(0, blocks // ahead, step, 0)

    prepare(own, 0, grid_real)
    prepare(other, blocks, grid_imag)

    def build(source, offset, block, slot):
        first_row = corner[offset + block, 0] // grid_size
        payload = source[block].astype(jnp.float32)
        row_weights = weight_y[offset + block]
        plane_weights = weight_x[offset + block]
        turn_real = jnp.zeros((YROWS, samples), jnp.float32)
        turn_imag = jnp.zeros((YROWS, samples), jnp.float32)
        for row in range(WIN):
            weight = row_weights[row : row + 1]
            turn_real = turn_real + cos_rows[first_row + row] * weight
            turn_imag = turn_imag + sin_rows[first_row + row] * weight
        by_plane = []
        for tap in range(0, TAPS, 2):
            by_plane.append(jnp.concatenate(
                [jnp.broadcast_to(plane_weights[at : at + 1], (YROWS, samples)) for at in (tap, tap + 1)],
                axis=0,
            ).astype(jnp.bfloat16))
        for coil in range(coils):
            amp_real = payload[2 * coil : 2 * coil + 1]
            amp_imag = payload[2 * coil + 1 : 2 * coil + 2]
            parts = (
                amp_real * turn_real - amp_imag * turn_imag,
                amp_real * turn_imag + amp_imag * turn_real,
            )
            for part, value in enumerate(parts):
                twice = jnp.concatenate([value, value], axis=0).astype(jnp.bfloat16)
                for pair, weight in enumerate(by_plane):
                    left[slot][
                        pl.ds(coil * TAPS * YROWS + pair * 2 * YROWS, 2 * YROWS),
                        pl.ds(part * samples, samples),
                    ] = twice * weight

    def spread(offset, block, slot):
        first_plane = lax.rem(corner[offset + block, 0], grid_size)
        product = lax.dot_general(
            left[slot][...], weights[offset + block], (((1,), (1,)), ((), ())),
            preferred_element_type=jnp.float32,
        )
        rows = TAPS * YROWS
        per = grid_real[0].shape[0]
        for coil in range(coils):
            at = pl.ds(pl.multiple_of(first_plane * YROWS, YROWS), rows)
            part = product[coil * rows : (coil + 1) * rows]
            real, imag = grid_real[coil // per], grid_imag[coil // per]
            real[coil % per, at, :] = real[coil % per, at, :] + part[:, :grid_size]
            imag[coil % per, at, :] = imag[coil % per, at, :] + part[:, grid_size:]

    def spread_planes(source, offset):
        build(source, offset, 0, 0)

        def step(index, carry):
            block = index * unroll
            for part in range(unroll):
                later = jnp.minimum(block + part + 1, blocks - 1)
                build(source, offset, later, (part + 1) % unroll)
                spread(offset, block + part, part)
            return carry

        lax.fori_loop(0, blocks // unroll, step, 0)

    corners.wait()
    spread_planes(own, 0)
    spread_planes(other, blocks)

    wrap = (TAPS - 1) * YROWS
    top = grid_size * YROWS
    for ref in grid_real + grid_imag:
        ref[:, :wrap, :] = ref[:, :wrap, :] + ref[:, top : top + wrap, :]

    for copy in copies:
        copy.wait()

    columns = weights
    pairs = coils // 2
    per = grid_real[0].shape[0]

    def transpose(step, carry):
        start = step * 16
        for coil in range(coils):
            lanes = slice((coil % 2) * grid_size, (coil % 2 + 1) * grid_size)
            for part, refs in enumerate((grid_real, grid_imag)):
                at = pl.ds(pl.multiple_of(start * YROWS, 16 * YROWS), 16 * YROWS)
                planes = refs[coil // per][coil % per, at, :].reshape(16, YROWS, grid_size)
                rows = jnp.swapaxes(planes, 0, 1).astype(jnp.bfloat16)
                at = pl.ds(pl.multiple_of(part * grid_size + start, 16), 16)
                for row in range(slab):
                    columns[row * pairs + coil // 2, at, lanes] = rows[row]
        return carry

    lax.fori_loop(0, grid_size // 16, transpose, 0)

    def image_row(row, carry):
        for quad in range(coils // 4):
            images = [
                jnp.dot(
                    plane_dft[...], columns[row * pairs + pair], preferred_element_type=jnp.float32
                )
                for pair in (2 * quad, 2 * quad + 1)
            ]
            for tile in range(grid_size // 16):
                at = pl.ds(tile * 16, 16)
                sums = [[], []]
                for place in range(4):
                    coil = 4 * quad + place
                    column = (place % 2) * grid_size
                    image = images[place // 2][tile * 32 : tile * 32 + 32, column : column + grid_size]
                    image_real = jnp.concatenate([image[:8], image[16:24]], axis=0)
                    image_imag = jnp.concatenate([image[8:16], image[24:]], axis=0)
                    map_real = maps[coil, 0, row, at].astype(jnp.float32)
                    map_imag = maps[coil, 1, row, at].astype(jnp.float32)
                    sums[0].append(map_real * image_real + map_imag * image_imag)
                    sums[1].append(map_real * image_imag - map_imag * image_real)
                for part in range(2):
                    value = (sums[part][0] + sums[part][1]) + (sums[part][2] + sums[part][3])
                    if quad > 0:
                        value = value + total[part, at]
                    if quad < coils // 4 - 1:
                        total[part, at] = value
                    else:
                        value = estimate[part, row, at] + scale * value
                        half[part, row, at] = value
                        if half_small is not None:
                            half_small[part, row, at] = value.astype(jnp.bfloat16)
        return carry

    lax.fori_loop(0, slab, image_row, 0)


def frame_image(own, other, plane_dft, coil_maps, estimate, scale, place, shared):
    blocks, _, samples = own.shape
    coils, _, slab, grid_size, _ = coil_maps.shape
    shape = (2, slab, grid_size, grid_size)
    whole = pl.BlockSpec(memory_space=pltpu.VMEM)
    away = pl.BlockSpec(memory_space=pltpu.HBM)
    unroll = math.gcd(blocks, UNROLL)
    grid_shape = (coils // math.gcd(coils, GROUPS), (grid_size + WIN) * YROWS, grid_size)
    outs = (jnp.float32, jnp.bfloat16)[: 2 if shared else 1]
    return pl.pallas_call(
        functools.partial(frame_kernel, place=place, scale=scale),
        out_shape=tuple(jax.ShapeDtypeStruct(shape, kind) for kind in outs),
        in_specs=[whole] * 2 + [away] * 3,
        out_specs=(whole,) * len(outs),
        scratch_shapes=[
            pltpu.VMEM((2 * grid_size, grid_size), jnp.bfloat16),
            pltpu.VMEM(plane_dft.shape, jnp.bfloat16),
            pltpu.VMEM((grid_size + WIN, YROWS, samples), jnp.float32),
            pltpu.VMEM((grid_size + WIN, YROWS, samples), jnp.float32),
            pltpu.VMEM((2 * blocks, samples), jnp.int32),
            pltpu.SMEM((2 * blocks, samples), jnp.int32),
            [pltpu.VMEM(grid_shape, jnp.float32)] * math.gcd(coils, GROUPS),
            [pltpu.VMEM(grid_shape, jnp.float32)] * math.gcd(coils, GROUPS),
            [pltpu.VMEM((coils * TAPS * YROWS, 2 * samples), jnp.bfloat16)] * unroll,
            pltpu.VMEM((2 * blocks, 2 * grid_size, 2 * samples), jnp.bfloat16),
            pltpu.VMEM((2 * blocks, 8, samples), jnp.float32),
            pltpu.VMEM((2 * blocks, 8, samples), jnp.float32),
            pltpu.VMEM(coil_maps.shape, jnp.bfloat16),
            pltpu.VMEM(shape, jnp.float32),
            pltpu.VMEM((2, grid_size, grid_size), jnp.float32),
            pltpu.SemaphoreType.DMA((4,)),
        ],
        compiler_params=pltpu.CompilerParams(vmem_limit_bytes=VMEM_LIMIT),
        cost_estimate=pl.CostEstimate(
            flops=2 * 2 * blocks * TAPS * coils * YROWS * 4 * samples * grid_size,
            bytes_accessed=coil_maps.size * 2,
            transcendentals=0,
        ),
    )(own, other, plane_dft, coil_maps, estimate)


def step_kernel(first, second, *rest):
    *besides, out_hbm, out, sems = rest
    index, count = lax.axis_index("frame"), lax.axis_size("frame")
    even = shared_first()
    place = jnp.where(even, 1, 0)
    there = (
        jnp.where(even, index + 1 < count, True),
        jnp.where(even, index > 0, index + 1 < count),
    )

    def slope(low, high):
        change = high - low
        return change * lax.rsqrt(change[0] * change[0] + change[1] * change[1] + EPS * EPS)[None]

    copies = []
    for row in range(out.shape[2]):
        values = first[:, row], second[:, row]
        pull = slope(values[0], values[1])
        pulls = [pull, -pull]
        for side, beside in enumerate(besides):
            outer = slope(values[side], beside[:, row].astype(jnp.float32))
            pulls[side] = pulls[side] + jnp.where(there[side], outer, 0.0)
        for side, at in enumerate((place, 1 - place)):
            out[side, :, row] = values[side] + LAMBDA_TV * pulls[side]
            copies.append(pltpu.make_async_copy(
                out.at[side, :, row], out_hbm.at[at, :, row], sems.at[side, row]
            ))
            copies[-1].start()
    for copy in copies:
        copy.wait()


def tv_step(halves, received):
    given = [value for value in received if value is not None]
    whole = pl.BlockSpec(memory_space=pltpu.VMEM)
    shape = (2,) + halves[0].shape
    return pl.pallas_call(
        step_kernel,
        out_shape=jax.ShapeDtypeStruct(shape, jnp.float32),
        in_specs=[whole] * (2 + len(given)),
        out_specs=pl.BlockSpec(memory_space=pltpu.HBM),
        scratch_shapes=[
            pltpu.VMEM(shape, jnp.float32),
            pltpu.SemaphoreType.DMA((2, shape[2])),
        ],
        compiler_params=pltpu.CompilerParams(vmem_limit_bytes=VMEM_LIMIT // 4),
    )(*halves, *given)


def swap(values, axis, bit):
    count = lax.axis_size(axis)
    return lax.ppermute(values, axis, [(index, index ^ bit) for index in range(count)])


def chips(held):
    shifts = range(2, lax.axis_size("tile") // 2, 2)
    return [held] + [swap(held, "tile", shift) for shift in shifts]


def on_device(
    kspace_samples, density, sample_frac, row_offsets, depth_base, block_base, coil_maps, estimate
):
    tile_count = lax.axis_size("tile")
    frame_count = lax.axis_size("frame")
    frames_local, blocks_local, channels, sample_count = kspace_samples.shape
    grid_size = coil_maps.shape[3]
    scale = 1.0 / (8.0 * math.sqrt(blocks_local * tile_count * sample_count))

    packed = pack_blocks(
        kspace_samples, density, sample_frac, row_offsets, depth_base, block_base
    )
    plane_dft = plane_table(grid_size)
    pairs = [
        [(index, index ^ 1) for index in range(frame_count) if index ^ 1 < frame_count],
        [(index, index - 1) for index in range(2, frame_count, 2)],
    ]
    pairs[1] += [(target, source) for source, target in pairs[1]]
    across = swap(packed, "tile", tile_count // 2)
    shared, rest = (
        jnp.concatenate([packed[place], across[place]], axis=0) for place in range(2)
    )
    shared = chips(shared)
    rest, *shared = lax.optimization_barrier((rest, *shared))
    held = [jnp.concatenate(shared, axis=0), chips(rest)]
    halves, received = [], []
    for place in range(2):
        if place == 1:
            (*pieces, halves[0]) = lax.optimization_barrier((*held[1], halves[0]))
            held[1] = jnp.concatenate(pieces, axis=0)
        half, *small = frame_image(
            held[place], swap(held[place], "tile", 1), plane_dft, coil_maps, estimate, scale, place,
            bool(pairs[place]),
        )
        halves.append(half)
        received.append(lax.ppermute(small[0], "frame", pairs[place]) if small else None)
    return tv_step(halves, received)


def solution(mesh):
    in_specs = (
        P("frame", "tile", None, None),
        P("frame", "tile", None),
        P("frame", "tile", None, None),
        P("frame", "tile", None),
        P("frame", "tile", None),
        P("frame", "tile", None),
        P(None, None, "tile", None, None),
        P("frame", None, "tile", None, None),
    )
    out_specs = P("frame", None, "tile", None, None)
    return jax.shard_map(
        on_device, mesh=mesh, in_specs=in_specs, out_specs=out_specs, check_vma=False
    )
```

```python
import functools
import math

import jax
import jax.numpy as jnp
import numpy as np
from jax import lax
from jax.experimental import pallas as pl
from jax.experimental.pallas import tpu as pltpu
from jax.sharding import PartitionSpec as P

TAPS = 6
WIN = 8
YROWS = 8
META = 8
BETA = 13.9
EPS = 0.05
LAMBDA_TV = 0.3
TERMS = 40
UNROLL = 16
AHEAD = 16
GROUPS = 16
LAST_REFS = 16
VMEM_LIMIT = 52 * 1024 * 1024


def kaiser_coefficients():
    quarter = BETA * BETA / 4.0
    terms = [quarter**power / math.factorial(power) ** 2 for power in range(TERMS)]
    total = math.fsum(terms)
    return [term / total for term in terms]


def kaiser(distance):
    coefficients = kaiser_coefficients()
    inside = jnp.maximum(1.0 - distance / 3.0 * (distance / 3.0), 0.0)
    value = jnp.full_like(inside, coefficients[-1])
    for coefficient in coefficients[-2::-1]:
        value = value * inside + coefficient
    return value


def dft_angles(grid_size):
    positions = np.arange(grid_size)
    return (positions[:, None] * positions[None, :] % grid_size) * (2.0 * math.pi / grid_size)


def plane_table(grid_size):
    angles = dft_angles(grid_size)
    cosine, sine = np.cos(angles), np.sin(angles)
    parts = np.stack([np.concatenate([cosine, -sine], 1), np.concatenate([sine, cosine], 1)])
    tiles = parts.reshape(2, grid_size // 8, 8, 2 * grid_size).swapaxes(0, 1)
    return jnp.asarray(tiles.reshape(2 * grid_size, 2 * grid_size), jnp.bfloat16)


def shared_first():
    return lax.rem(lax.axis_index("frame"), 2) == 0


def pack_kernel(samples, density, fractions, shift, depth, corner, packed):
    frames, blocks, _, count = samples.shape
    last = frames - 1
    for place in range(frames):
        frame = jnp.where(shared_first(), last - place, place)
        rows = [
            density[frame].astype(jnp.float32)[:, None],
            jnp.swapaxes(fractions[frame].astype(jnp.float32), 0, 1),
            shift[frame].astype(jnp.float32)[:, None],
            depth[frame].astype(jnp.float32)[:, None],
        ]
        for block in range(blocks):
            ends = [
                jnp.full((1, count), corner[frame, axis, block], jnp.int32).astype(jnp.float32)
                for axis in range(2)
            ]
            parts = [samples[frame, block].astype(jnp.float32)] + [row[block] for row in rows] + ends
            packed[place, block] = jnp.concatenate(parts, axis=0).astype(jnp.bfloat16)


def pack_blocks(samples, density, fractions, shift, depth, corner):
    frames, blocks, channels, count = samples.shape
    whole = pl.BlockSpec(memory_space=pltpu.VMEM)
    return pl.pallas_call(
        pack_kernel,
        out_shape=jax.ShapeDtypeStruct((frames, blocks, channels + META, count), jnp.bfloat16),
        in_specs=[whole] * 5 + [pl.BlockSpec(memory_space=pltpu.SMEM)],
        out_specs=whole,
    )(samples, density, jnp.swapaxes(fractions, 1, 2), shift, depth, jnp.swapaxes(corner, 1, 2))


def frame_kernel(
    own, other, plane_hbm, maps_hbm, estimate_hbm, half, *rest, place, scale,
):
    half_small = rest[0] if len(rest) == LAST_REFS + 1 else None
    frame_body(
        own, other, plane_hbm, maps_hbm, estimate_hbm, half, half_small,
        *rest[-LAST_REFS:], place=place, scale=scale,
    )


def frame_body(
    own, other, plane_hbm, maps_hbm, estimate_hbm, half, half_small,
    depth_dft, plane_dft, cos_rows, sin_rows, corner_rows, corner,
    grid_real, grid_imag, left, weights, weight_x, weight_y, maps, estimate, total, sems,
    *, place, scale,
):
    blocks = own.shape[0]
    samples = own.shape[2]
    unroll = len(left)
    coils, _, slab, grid_size, _ = maps.shape
    frame = jnp.where(shared_first(), estimate_hbm.shape[0] - 1 - place, place)
    copies = [
        pltpu.make_async_copy(maps_hbm, maps, sems.at[0]),
        pltpu.make_async_copy(estimate_hbm.at[frame], estimate, sems.at[1]),
    ]
    planes = pltpu.make_async_copy(plane_hbm, plane_dft, sems.at[2])
    planes.start()
    for copy in copies:
        copy.start()
    for source, offset in ((own, 0), (other, blocks)):
        for block in range(blocks):
            ends = source[block].astype(jnp.float32)[2 * coils + META - 2 :]
            corner_rows[pl.ds(offset + block, 1), :] = (ends[:1] + grid_size * ends[1:]).astype(jnp.int32)
    corners = pltpu.make_async_copy(corner_rows, corner, sems.at[3])
    corners.start()
    lanes = -(-(grid_size + WIN) // 128) * 128
    position = lax.broadcasted_iota(jnp.int32, (YROWS, lanes), 1)
    image_y = lax.axis_index("tile") * slab + lax.broadcasted_iota(jnp.int32, (YROWS, lanes), 0)
    angles = lax.rem(position * image_y, grid_size).astype(jnp.float32) * (2.0 * math.pi / grid_size)
    phases = jnp.cos(angles), jnp.sin(angles)
    stride = 16
    turn, *chain = (
        tuple(jnp.broadcast_to(phase[:, k : k + 1], (YROWS, samples)) for phase in phases)
        for k in (stride, *range(stride))
    )
    for k in range(grid_size + WIN):
        real, imag = chain[k % stride]
        cos_rows[k], sin_rows[k] = real, imag
        chain[k % stride] = real * turn[0] - imag * turn[1], real * turn[1] + imag * turn[0]
    planes.wait()
    tiles = plane_dft[:, :grid_size].astype(jnp.float32).reshape(grid_size // 8, 2, 8, grid_size)
    for part in range(2):
        at = slice(part * grid_size, (part + 1) * grid_size)
        depth_dft[at, :] = tiles[:, part].reshape(grid_size, grid_size).astype(jnp.bfloat16)

    table = depth_dft[...]
    taps = lax.broadcasted_iota(jnp.int32, (8, 2 * samples), 0).astype(jnp.float32)
    cells = lax.broadcasted_iota(jnp.int32, (grid_size, 2 * samples), 0).astype(jnp.bfloat16)
    ahead = math.gcd(blocks, AHEAD)
    clear_rows = grid_real[0].shape[1] // (blocks // ahead)

    def prepare(source, offset, cleared):
        def two(first):
            meta = jnp.concatenate(
                [source[first + part].astype(jnp.float32)[2 * coils :] for part in range(2)], axis=1
            )
            density, frac_x, frac_y, frac_z, shift, depth = (meta[row : row + 1] for row in range(6))
            tap_x = kaiser(taps - 2.0 - frac_x) * density
            lag = taps - shift
            tap_y = jnp.where((lag >= 0.0) & (lag < float(TAPS)), kaiser(lag - 2.0 - frac_y), 0.0)
            tap_z = kaiser(taps - 2.0 - frac_z).astype(jnp.bfloat16)
            cell = depth + taps
            cell = jnp.where(cell >= float(grid_size), cell - float(grid_size), cell)
            cell = cell.astype(jnp.bfloat16)
            spread = jnp.zeros((grid_size, 2 * samples), jnp.bfloat16)
            for tap in range(TAPS):
                spread = jnp.where(cells == cell[tap : tap + 1], tap_z[tap : tap + 1], spread)
            turned = jnp.dot(table, spread, preferred_element_type=jnp.float32).astype(jnp.bfloat16)
            real, imag = turned[:grid_size], turned[grid_size:]
            for part in range(2):
                at, here = offset + first + part, slice(part * samples, (part + 1) * samples)
                weight_x[at] = tap_x[:, here]
                weight_y[at] = tap_y[:, here]
                weights[at, :, :samples] = turned[:, here]
                weights[at, :grid_size, samples:] = -imag[:, here]
                weights[at, grid_size:, samples:] = real[:, here]

        def step(index, carry):
            for ref in cleared:
                at = pl.ds(pl.multiple_of(index * clear_rows, 8), clear_rows)
                ref[:, at, :] = jnp.zeros((ref.shape[0], clear_rows, grid_size), jnp.float32)
            for part in range(0, ahead, 2):
                two(index * ahead + part)
            return carry

        lax.fori_loop(0, blocks // ahead, step, 0)

    prepare(own, 0, grid_real)
    prepare(other, blocks, grid_imag)

    def build(source, offset, block, slot):
        first_row = corner[offset + block, 0] // grid_size
        payload = source[block].astype(jnp.float32)
        row_weights = weight_y[offset + block]
        plane_weights = weight_x[offset + block]
        turn_real = jnp.zeros((YROWS, samples), jnp.float32)
        turn_imag = jnp.zeros((YROWS, samples), jnp.float32)
        for row in range(WIN):
            weight = row_weights[row : row + 1]
            turn_real = turn_real + cos_rows[first_row + row] * weight
            turn_imag = turn_imag + sin_rows[first_row + row] * weight
        by_plane = []
        for tap in range(0, TAPS, 2):
            by_plane.append(jnp.concatenate(
                [jnp.broadcast_to(plane_weights[at : at + 1], (YROWS, samples)) for at in (tap, tap + 1)],
                axis=0,
            ).astype(jnp.bfloat16))
        for coil in range(coils):
            amp_real = payload[2 * coil : 2 * coil + 1]
            amp_imag = payload[2 * coil + 1 : 2 * coil + 2]
            parts = (
                amp_real * turn_real - amp_imag * turn_imag,
                amp_real * turn_imag + amp_imag * turn_real,
            )
            for part, value in enumerate(parts):
                twice = jnp.concatenate([value, value], axis=0).astype(jnp.bfloat16)
                for pair, weight in enumerate(by_plane):
                    left[slot][
                        pl.ds(coil * TAPS * YROWS + pair * 2 * YROWS, 2 * YROWS),
                        pl.ds(part * samples, samples),
                    ] = twice * weight

    def spread(offset, block, slot):
        first_plane = lax.rem(corner[offset + block, 0], grid_size)
        product = lax.dot_general(
            left[slot][...], weights[offset + block], (((1,), (1,)), ((), ())),
            preferred_element_type=jnp.float32,
        )
        rows = TAPS * YROWS
        per = grid_real[0].shape[0]
        for coil in range(coils):
            at = pl.ds(pl.multiple_of(first_plane * YROWS, YROWS), rows)
            part = product[coil * rows : (coil + 1) * rows]
            real, imag = grid_real[coil // per], grid_imag[coil // per]
            real[coil % per, at, :] = real[coil % per, at, :] + part[:, :grid_size]
            imag[coil % per, at, :] = imag[coil % per, at, :] + part[:, grid_size:]

    def spread_planes(source, offset):
        build(source, offset, 0, 0)

        def step(index, carry):
            block = index * unroll
            for part in range(unroll):
                later = jnp.minimum(block + part + 1, blocks - 1)
                build(source, offset, later, (part + 1) % unroll)
                spread(offset, block + part, part)
            return carry

        lax.fori_loop(0, blocks // unroll, step, 0)

    corners.wait()
    spread_planes(own, 0)
    spread_planes(other, blocks)

    wrap = (TAPS - 1) * YROWS
    top = grid_size * YROWS
    for ref in grid_real + grid_imag:
        ref[:, :wrap, :] = ref[:, :wrap, :] + ref[:, top : top + wrap, :]

    for copy in copies:
        copy.wait()

    columns = weights
    pairs = coils // 2
    per = grid_real[0].shape[0]

    def transpose(step, carry):
        start = step * 16
        for coil in range(coils):
            lanes = slice((coil % 2) * grid_size, (coil % 2 + 1) * grid_size)
            for part, refs in enumerate((grid_real, grid_imag)):
                at = pl.ds(pl.multiple_of(start * YROWS, 16 * YROWS), 16 * YROWS)
                planes = refs[coil // per][coil % per, at, :].reshape(16, YROWS, grid_size)
                rows = jnp.swapaxes(planes, 0, 1).astype(jnp.bfloat16)
                at = pl.ds(pl.multiple_of(part * grid_size + start, 16), 16)
                for row in range(slab):
                    columns[row * pairs + coil // 2, at, lanes] = rows[row]
        return carry

    lax.fori_loop(0, grid_size // 16, transpose, 0)

    def image_row(row, carry):
        for quad in range(coils // 4):
            images = [
                jnp.dot(
                    plane_dft[...], columns[row * pairs + pair], preferred_element_type=jnp.float32
                )
                for pair in (2 * quad, 2 * quad + 1)
            ]
            for tile in range(grid_size // 16):
                at = pl.ds(tile * 16, 16)
                sums = [[], []]
                for place in range(4):
                    coil = 4 * quad + place
                    column = (place % 2) * grid_size
                    image = images[place // 2][tile * 32 : tile * 32 + 32, column : column + grid_size]
                    image_real = jnp.concatenate([image[:8], image[16:24]], axis=0)
                    image_imag = jnp.concatenate([image[8:16], image[24:]], axis=0)
                    map_real = maps[coil, 0, row, at].astype(jnp.float32)
                    map_imag = maps[coil, 1, row, at].astype(jnp.float32)
                    sums[0].append(map_real * image_real + map_imag * image_imag)
                    sums[1].append(map_real * image_imag - map_imag * image_real)
                for part in range(2):
                    value = (sums[part][0] + sums[part][1]) + (sums[part][2] + sums[part][3])
                    if quad > 0:
                        value = value + total[part, at]
                    if quad < coils // 4 - 1:
                        total[part, at] = value
                    else:
                        value = estimate[part, row, at] + scale * value
                        half[part, row, at] = value
                        if half_small is not None:
                            half_small[part, row, at] = value.astype(jnp.bfloat16)
        return carry

    lax.fori_loop(0, slab, image_row, 0, unroll=2)


def frame_image(own, other, plane_dft, coil_maps, estimate, scale, place, shared):
    blocks, _, samples = own.shape
    coils, _, slab, grid_size, _ = coil_maps.shape
    shape = (2, slab, grid_size, grid_size)
    whole = pl.BlockSpec(memory_space=pltpu.VMEM)
    away = pl.BlockSpec(memory_space=pltpu.HBM)
    unroll = math.gcd(blocks, UNROLL)
    grid_shape = (coils // math.gcd(coils, GROUPS), (grid_size + WIN) * YROWS, grid_size)
    outs = (jnp.float32, jnp.bfloat16)[: 2 if shared else 1]
    return pl.pallas_call(
        functools.partial(frame_kernel, place=place, scale=scale),
        out_shape=tuple(jax.ShapeDtypeStruct(shape, kind) for kind in outs),
        in_specs=[whole] * 2 + [away] * 3,
        out_specs=(whole,) * len(outs),
        scratch_shapes=[
            pltpu.VMEM((2 * grid_size, grid_size), jnp.bfloat16),
            pltpu.VMEM(plane_dft.shape, jnp.bfloat16),
            pltpu.VMEM((grid_size + WIN, YROWS, samples), jnp.float32),
            pltpu.VMEM((grid_size + WIN, YROWS, samples), jnp.float32),
            pltpu.VMEM((2 * blocks, samples), jnp.int32),
            pltpu.SMEM((2 * blocks, samples), jnp.int32),
            [pltpu.VMEM(grid_shape, jnp.float32)] * math.gcd(coils, GROUPS),
            [pltpu.VMEM(grid_shape, jnp.float32)] * math.gcd(coils, GROUPS),
            [pltpu.VMEM((coils * TAPS * YROWS, 2 * samples), jnp.bfloat16)] * unroll,
            pltpu.VMEM((2 * blocks, 2 * grid_size, 2 * samples), jnp.bfloat16),
            pltpu.VMEM((2 * blocks, 8, samples), jnp.float32),
            pltpu.VMEM((2 * blocks, 8, samples), jnp.float32),
            pltpu.VMEM(coil_maps.shape, jnp.bfloat16),
            pltpu.VMEM(shape, jnp.float32),
            pltpu.VMEM((2, grid_size, grid_size), jnp.float32),
            pltpu.SemaphoreType.DMA((4,)),
        ],
        compiler_params=pltpu.CompilerParams(vmem_limit_bytes=VMEM_LIMIT),
        cost_estimate=pl.CostEstimate(
            flops=2 * 2 * blocks * TAPS * coils * YROWS * 4 * samples * grid_size,
            bytes_accessed=coil_maps.size * 2,
            transcendentals=0,
        ),
    )(own, other, plane_dft, coil_maps, estimate)


def step_kernel(first, second, *rest):
    *besides, out_hbm, out, sems = rest
    index, count = lax.axis_index("frame"), lax.axis_size("frame")
    even = shared_first()
    place = jnp.where(even, 1, 0)
    there = (
        jnp.where(even, index + 1 < count, True),
        jnp.where(even, index > 0, index + 1 < count),
    )

    def slope(low, high):
        change = high - low
        return change * lax.rsqrt(change[0] * change[0] + change[1] * change[1] + EPS * EPS)[None]

    copies = []
    for row in range(out.shape[2]):
        values = first[:, row], second[:, row]
        pull = slope(values[0], values[1])
        pulls = [pull, -pull]
        for side, beside in enumerate(besides):
            outer = slope(values[side], beside[:, row].astype(jnp.float32))
            pulls[side] = pulls[side] + jnp.where(there[side], outer, 0.0)
        for side, at in enumerate((place, 1 - place)):
            out[side, :, row] = values[side] + LAMBDA_TV * pulls[side]
            copies.append(pltpu.make_async_copy(
                out.at[side, :, row], out_hbm.at[at, :, row], sems.at[side, row]
            ))
            copies[-1].start()
    for copy in copies:
        copy.wait()


def tv_step(halves, received):
    given = [value for value in received if value is not None]
    whole = pl.BlockSpec(memory_space=pltpu.VMEM)
    shape = (2,) + halves[0].shape
    return pl.pallas_call(
        step_kernel,
        out_shape=jax.ShapeDtypeStruct(shape, jnp.float32),
        in_specs=[whole] * (2 + len(given)),
        out_specs=pl.BlockSpec(memory_space=pltpu.HBM),
        scratch_shapes=[
            pltpu.VMEM(shape, jnp.float32),
            pltpu.SemaphoreType.DMA((2, shape[2])),
        ],
        compiler_params=pltpu.CompilerParams(vmem_limit_bytes=VMEM_LIMIT // 4),
    )(*halves, *given)


def swap(values, axis, bit):
    count = lax.axis_size(axis)
    return lax.ppermute(values, axis, [(index, index ^ bit) for index in range(count)])


def chips(held):
    shifts = range(2, lax.axis_size("tile") // 2, 2)
    return [held] + [swap(held, "tile", shift) for shift in shifts]


def on_device(
    kspace_samples, density, sample_frac, row_offsets, depth_base, block_base, coil_maps, estimate
):
    tile_count = lax.axis_size("tile")
    frame_count = lax.axis_size("frame")
    frames_local, blocks_local, channels, sample_count = kspace_samples.shape
    grid_size = coil_maps.shape[3]
    scale = 1.0 / (8.0 * math.sqrt(blocks_local * tile_count * sample_count))

    packed = pack_blocks(
        kspace_samples, density, sample_frac, row_offsets, depth_base, block_base
    )
    plane_dft = plane_table(grid_size)
    pairs = [
        [(index, index ^ 1) for index in range(frame_count) if index ^ 1 < frame_count],
        [(index, index - 1) for index in range(2, frame_count, 2)],
    ]
    pairs[1] += [(target, source) for source, target in pairs[1]]
    across = swap(packed, "tile", tile_count // 2)
    shared, rest = (
        jnp.concatenate([packed[place], across[place]], axis=0) for place in range(2)
    )
    shared = chips(shared)
    rest, *shared = lax.optimization_barrier((rest, *shared))
    held = [jnp.concatenate(shared, axis=0), chips(rest)]
    halves, received = [], []
    for place in range(2):
        if place == 1:
            (*pieces, halves[0]) = lax.optimization_barrier((*held[1], halves[0]))
            held[1] = jnp.concatenate(pieces, axis=0)
        half, *small = frame_image(
            held[place], swap(held[place], "tile", 1), plane_dft, coil_maps, estimate, scale, place,
            bool(pairs[place]),
        )
        halves.append(half)
        received.append(lax.ppermute(small[0], "frame", pairs[place]) if small else None)
    return tv_step(halves, received)


def solution(mesh):
    in_specs = (
        P("frame", "tile", None, None),
        P("frame", "tile", None),
        P("frame", "tile", None, None),
        P("frame", "tile", None),
        P("frame", "tile", None),
        P("frame", "tile", None),
        P(None, None, "tile", None, None),
        P("frame", None, "tile", None, None),
    )
    out_specs = P("frame", None, "tile", None, None)
    return jax.shard_map(
        on_device, mesh=mesh, in_specs=in_specs, out_specs=out_specs, check_vma=False
    )
```
